32 devices in a mesh: leaf: 8 (over z, y), front: 4 (over x, core).
Axes of the slice: x: 2, y: 2, z: 4, core: 2. Of those that a mesh axis runs over, the one named last changes fastest.
Arguments:
- sub_rhs: float32 [98304, 128], P(('leaf', 'front')), may hold values from -6 to 6
- sub_dinv: float32 [768, 128, 128], P(('leaf', 'front')), as said below
- sub_off: float32 [736, 2, 128, 128], P(('leaf', 'front')), may hold values from -0.25 to 0.25
- sub_pattern: int32 [736, 2], P(('leaf', 'front')), may hold values from 0 to 22, as said below
- sub_update: float32 [8192, 3072], P(('leaf', 'front')), may hold values from -0.0546875 to 0.0546875
- sub_map: int32 [32, 2], replicated, may hold values from 0 to 31, as said below
- front_rhs: float32 [30720, 128], P(('leaf', 'front')), may hold values from -6 to 6
- piv_inverse: float32 [30720, 2048], P(('leaf', 'front')), as said below
- upd_factor: float32 [28672, 2048], P(('leaf', 'front')), may hold values from -0.0625 to 0.0625
- front_map: int32 [14, 16], replicated, may hold values from 0 to 31, as said below
Outputs:
- sub_solution: float32 [98304, 128], P(('leaf', 'front'))
- front_solution: float32 [30720, 128], P(('leaf', 'front'))
The draws below stay inside these ranges and needn't reach their ends.
Inputs may be any that keep to these rules, and one draw needn't show every extreme that they name: `sub_pattern`: in entry row i - 1 of a subtree (its block row i) the first index is i - 1 and every index is below i. `sub_map`: each row names 2 different blocks of a level-1 front. `front_map`: rows are ordered by level, then by front; each row names 16 different parent blocks, and the last two rows (children of the root) name only the 16 pivot blocks. `sub_dinv`: each inverse diagonal block is full. `piv_inverse`: each front's inverse pivot block is lower triangular with a unit diagonal.
All inputs are finite; a program needn't handle non-finite values.
Results may differ from the reference program's by a relative error of at most 0.0001.
Values sent between devices are 32-bit elements; how exact they have to be, the bound alone decides.
No kernel may reach another device: no remote copies, remote signals or barrier semaphores. Data moves between devices by JAX's collectives and lax.ppermute only.
A program may use at most 128 MiB of HBM per device.

```python
import math
import jax
import jax.numpy as jnp
from jax import lax

B = 128
NRHS = 128
P_SIZE = 2048
U = 2048
SB = 24
USB = 2
K = 2
LEVELS = 4
PB = 16
UB = 16
PROWS = 960
UROWS = 896
MAPROWS = 14
N_LEAF = 8
N_FRONT = 4


def draw_sub_dinv(key, part):
    shape = (N_LEAF * N_FRONT * SB, B, B)
    noise_values = jax.random.normal(key, shape, jnp.float32)
    return jnp.eye(B, dtype=jnp.float32)[None, :, :] + 0.35 * noise_values / math.sqrt(B)


def draw_piv_inverse(key, part):
    total = N_LEAF * N_FRONT * PROWS
    row_ids = jnp.arange(total)
    device_ids = row_ids // PROWS
    local_row = row_ids % PROWS
    leaf_ids = device_ids // N_FRONT
    front_ids = device_ids % N_FRONT
    node_row = jnp.zeros((total,), jnp.int32)
    offset = 0
    for level in range(1, LEVELS + 1):
        group_span = 2 ** (level - 1)
        piv_rows = P_SIZE // (N_FRONT * group_span)
        inside = (local_row >= offset) & (local_row < offset + piv_rows)
        my_rank = leaf_ids % group_span * N_FRONT + front_ids
        node_row = jnp.where(inside, my_rank * piv_rows + local_row - offset, node_row)
        offset += piv_rows
    column_ids = jnp.arange(P_SIZE)
    noise_values = jax.random.normal(key, (total, P_SIZE), jnp.float32)
    noise_values = noise_values / math.sqrt(P_SIZE)
    lower = column_ids[None, :] < node_row[:, None]
    diagonal = (column_ids[None, :] == node_row[:, None]).astype(jnp.float32)
    return jnp.where(lower, noise_values, 0.0) + diagonal


def draw_sub_pattern(key, part):
    total = N_LEAF * N_FRONT * (SB - 1)
    block_row = jnp.arange(total) % (SB - 1) + 1
    others = jax.random.randint(key, (total, K - 1), 0, block_row[:, None])
    return jnp.concatenate([(block_row - 1)[:, None], others], axis=1).astype(jnp.int32)


def distinct_blocks(key, count_rows, limit_rows):
    scores = jax.random.randint(key, (count_rows, PB + UB), 0, 2 ** 20)
    positions = jnp.arange(PB + UB)
    scores = scores * (PB + UB) + positions[None, :]
    scores = jnp.where((positions[None, :] >= PB) & limit_rows[:, None], scores + 2 ** 30, scores)
    ordering = jnp.argsort(scores, axis=1, stable=True)
    return ordering.astype(jnp.int32)


def draw_sub_map(key, part):
    count_rows = N_LEAF * N_FRONT
    ordering = distinct_blocks(jax.random.fold_in(key, 11), count_rows, jnp.zeros((count_rows,), bool))
    return ordering[:, :USB]


def draw_front_map(key, part):
    count_rows = MAPROWS
    limit_rows = jnp.arange(count_rows) >= count_rows - 2
    ordering = distinct_blocks(jax.random.fold_in(key, 23), count_rows, limit_rows)
    return ordering[:, :UB]


def levels(stream_key, extent, cuts, smallest, top_value):
    def one(axis_at, shards_of):
        draws = jax.random.uniform(jax.random.fold_in(jax.random.fold_in(stream_key, 6), axis_at), (shards_of,), jnp.float32, smallest / len(cuts), top_value / len(cuts))
        return jnp.repeat(jnp.exp(draws), extent[axis_at] // shards_of).reshape((-1,) + (1,) * (len(extent) - axis_at - 1))

    loudness = one(*cuts[0])
    for cut in cuts[1:]:
        loudness = loudness * one(*cut)
    return loudness


def gaussian(stream_key, dims, width, most, pieces=(), kind=jnp.bfloat16):
    values = jax.random.normal(stream_key, dims, jnp.float32) * width
    if len(pieces) > 0:
        values = levels(stream_key, dims, pieces, -0.22, 0.18) * values
    return jnp.clip(values, min=-most, max=most).astype(kind)


def setup_inputs(seed: int = 0) -> dict:
    key_of = jax.random.split(jax.random.key(seed), 11)
    sub_rhs = gaussian(key_of[0], (N_LEAF * N_FRONT * SB * B, NRHS), 1.0, 6.0, ((0, 32),), jnp.float32)
    sub_dinv = draw_sub_dinv(jax.random.fold_in(key_of[10], 71), 0)
    sub_off = gaussian(key_of[2], (N_LEAF * N_FRONT * (SB - 1), K, B, B), (2 * K * B) ** -0.5, 0.25, ((0, 32),), jnp.float32)
    sub_pattern = draw_sub_pattern(jax.random.fold_in(key_of[10], 71), 0)
    sub_update = gaussian(key_of[4], (N_LEAF * N_FRONT * USB * B, SB * B), (4 * SB * B) ** -0.5, 0.0546875, ((0, 32),), jnp.float32)
    sub_map = draw_sub_map(jax.random.fold_in(key_of[10], 71), 0)
    front_rhs = gaussian(key_of[6], (N_LEAF * N_FRONT * PROWS, NRHS), 1.0, 6.0, ((0, 32),), jnp.float32)
    piv_inverse = draw_piv_inverse(jax.random.fold_in(key_of[10], 71), 0)
    upd_factor = gaussian(key_of[8], (N_LEAF * N_FRONT * UROWS, P_SIZE), (4 * P_SIZE) ** -0.5, 0.0625, ((0, 32),), jnp.float32)
    front_map = draw_front_map(jax.random.fold_in(key_of[10], 71), 0)
    return {"sub_rhs": sub_rhs, "sub_dinv": sub_dinv, "sub_off": sub_off, "sub_pattern": sub_pattern, "sub_update": sub_update, "sub_map": sub_map, "front_rhs": front_rhs, "piv_inverse": piv_inverse, "upd_factor": upd_factor, "front_map": front_map}


def solve_subtree(operands):
    right_side, diag_inverse, off_blocks, pattern, update_rows = operands
    highest = lax.Precision.HIGHEST
    blocks = right_side.reshape(SB, B, NRHS)
    solved = jnp.zeros((SB, B, NRHS), jnp.float32)
    solved = solved.at[0].set(jnp.dot(diag_inverse[0], blocks[0], precision=highest, preferred_element_type=jnp.float32))

    def advance(block_id, solved):
        remain = blocks[block_id]
        for which in range(K):
            remain = remain - jnp.dot(off_blocks[block_id - 1, which], solved[pattern[block_id - 1, which]], precision=highest, preferred_element_type=jnp.float32)
        return solved.at[block_id].set(jnp.dot(diag_inverse[block_id], remain, precision=highest, preferred_element_type=jnp.float32))

    solved = lax.fori_loop(1, SB, advance, solved)
    flat_rows = solved.reshape(SB * B, NRHS)
    return flat_rows, -jnp.dot(update_rows, flat_rows, precision=highest, preferred_element_type=jnp.float32)


def take_level(array, offset, count, num_nodes, group_span):
    piece = array[:, :, offset:offset + count]
    return piece.reshape(num_nodes, group_span * N_FRONT * count, array.shape[3])


def reference(sub_rhs, sub_dinv, sub_off, sub_pattern, sub_update, sub_map, front_rhs, piv_inverse, upd_factor, front_map):
    highest = lax.Precision.HIGHEST
    devices_all = N_LEAF * N_FRONT
    sub_y, sub_w = lax.map(solve_subtree, (sub_rhs.reshape(devices_all, SB * B, NRHS), sub_dinv.reshape(devices_all, SB, B, B), sub_off.reshape(devices_all, SB - 1, K, B, B), sub_pattern.reshape(devices_all, SB - 1, K), sub_update.reshape(devices_all, USB * B, SB * B)))
    child_blocks = sub_w.reshape(N_LEAF, N_FRONT * USB, B, NRHS)
    child_maps = sub_map.reshape(N_LEAF, N_FRONT * USB)
    onehot = (child_maps[:, :, None] == jnp.arange(PB + UB)[None, None, :]).astype(jnp.float32)
    contrib = jnp.einsum('ncb,ncrs->nbrs', onehot, child_blocks, precision=highest).reshape(N_LEAF, (PB + UB) * B, NRHS)
    rhs_view = front_rhs.reshape(N_LEAF, N_FRONT, PROWS, NRHS)
    piv_view = piv_inverse.reshape(N_LEAF, N_FRONT, PROWS, P_SIZE)
    upd_view = upd_factor.reshape(N_LEAF, N_FRONT, UROWS, P_SIZE)
    results = []
    piv_offset = 0
    upd_offset = 0
    map_offset = 0
    for level in range(1, LEVELS + 1):
        group_span = 2 ** (level - 1)
        num_nodes = N_LEAF // group_span
        piv_rows = P_SIZE // (N_FRONT * group_span)
        pivot_side = take_level(rhs_view, piv_offset, piv_rows, num_nodes, group_span) + contrib[:, :P_SIZE]
        update_side = contrib[:, P_SIZE:]
        inverse_rows = take_level(piv_view, piv_offset, piv_rows, num_nodes, group_span)
        solution = jnp.einsum('nij,njs->nis', inverse_rows, pivot_side, precision=highest)
        results.append(solution.reshape(N_LEAF, N_FRONT, piv_rows, NRHS))
        if level < LEVELS:
            upd_rows = U // (N_FRONT * group_span)
            factor_rows = take_level(upd_view, upd_offset, upd_rows, num_nodes, group_span)
            update = update_side - jnp.einsum('nij,njs->nis', factor_rows, solution, precision=highest)
            parent_blocks = PB + UB if level + 1 < LEVELS else PB
            level_maps = front_map[map_offset:map_offset + num_nodes]
            onehot = (level_maps[:, :, None] == jnp.arange(parent_blocks)[None, None, :]).astype(jnp.float32)
            placed = jnp.einsum('ncb,ncrs->nbrs', onehot, update.reshape(num_nodes, UB, B, NRHS), precision=highest)
            contrib = placed.reshape(num_nodes // 2, 2, parent_blocks * B, NRHS).sum(axis=1)
            upd_offset += upd_rows
            map_offset += num_nodes
        piv_offset += piv_rows
    front_solution = jnp.concatenate(results, axis=2).reshape(N_LEAF * N_FRONT * PROWS, NRHS)
    return sub_y.reshape(N_LEAF * N_FRONT * SB * B, NRHS), front_solution
```

```python
import functools

import jax
import jax.numpy as jnp
from jax import lax
from jax.experimental import pallas as pl
from jax.experimental.pallas import tpu as pltpu
from jax.sharding import PartitionSpec as P

AXES = ("leaf", "front")
B = 128
BF16 = jnp.bfloat16
F32 = jnp.float32
VMEM = pl.BlockSpec(memory_space=pltpu.VMEM)
SMEM = pl.BlockSpec(memory_space=pltpu.SMEM)
MIB = 2**20


def halves(x):
    high = x.astype(BF16)
    return high, (x - high.astype(F32)).astype(BF16)


def tall(x):
    return jnp.concatenate(halves(x), 0)


def wide(x):
    return jnp.concatenate(halves(x), 1)


def product(left, right):
    both = jnp.dot(left, right, preferred_element_type=F32)
    rows, cols = left.shape[0] // 2, right.shape[1] // 2
    return both[:rows, :cols] + both[:rows, cols:] + both[rows:, :cols]


def subtree_kernel(pattern, rhs, dinv, off, upd, y, w, coef, lead, solved):
    count = dinv.shape[0]

    def put(i, value):
        rows = pl.ds(i * B, B)
        y[rows, :] = value
        solved[rows, :] = wide(value)

    def prepare(i):
        right = jnp.concatenate([off[i - 1, 0], off[i - 1, 1], rhs[pl.ds(i * B, B), :]], 1)
        out = product(tall(dinv[i]), wide(right))
        lead[i] = out[:, 2 * B :]
        coef[i] = tall(-out[:, : 2 * B])

    def step(i):
        first = pl.multiple_of(pattern[i - 1, 0] * B, B)
        second = pl.multiple_of(pattern[i - 1, 1] * B, B)
        known = jnp.concatenate([solved[pl.ds(first, B), :], solved[pl.ds(second, B), :]], 0)
        put(i, lead[i] + product(coef[i], known))

    put(0, product(tall(dinv[0]), wide(rhs[:B, :])))
    prepare(1)
    for i in range(1, count):
        if i + 1 < count:
            prepare(i + 1)
        step(i)
    w[...] = -product(tall(upd[...]), solved[...])


def solve_subtree(rhs, dinv, off, pattern, upd):
    count = dinv.shape[0]
    return pl.pallas_call(
        subtree_kernel,
        out_shape=(
            jax.ShapeDtypeStruct(rhs.shape, F32),
            jax.ShapeDtypeStruct((upd.shape[0], rhs.shape[1]), F32),
        ),
        in_specs=[SMEM, VMEM, VMEM, VMEM, VMEM],
        out_specs=(VMEM, VMEM),
        scratch_shapes=[
            pltpu.VMEM((count, 2 * B, 2 * B), BF16),
            pltpu.VMEM((count, B, B), F32),
            pltpu.VMEM((count * B, 2 * B), BF16),
        ],
        compiler_params=pltpu.CompilerParams(vmem_limit_bytes=40 * MIB),
        cost_estimate=pl.CostEstimate(flops=2 * 10**9, bytes_accessed=12 * 10**6, transcendentals=0),
        name="subtree",
    )(pattern, rhs, dinv, off, upd)


def exchange(x, mask):
    size = lax.axis_size("leaf") * lax.axis_size("front")
    return lax.ppermute(x, AXES, [(source, source ^ mask) for source in range(size)])


def spread(x, group):
    masks = [0]
    apart = group // 2
    while apart >= 16:
        x = jnp.concatenate([x, exchange(x, apart)], 0)
        masks = masks + [mask ^ apart for mask in masks]
        apart //= 2
    low = 2 * apart
    arrays = [(0, x)]
    for mask in range(low - 2, 0, -2):
        arrays.append((mask, exchange(x, mask)))
    arrays += [(mask ^ 1, exchange(array, 1)) for mask, array in arrays]
    return [(array, [mask ^ high for high in masks]) for mask, array in arrays]


def pivot_kernel(masks, shape, me, maps, *refs):
    count = len(masks)
    pieces = refs[:count]
    h, factor = refs[count : count + 2]
    earlier = refs[count + 2 : count + 2 + shape["earlier"]]
    rest = refs[count + 2 + shape["earlier"] :]
    front = shape["front"]
    p_size, child_rows, span = shape["p_size"], shape["child_rows"], shape["child_span"]
    upd_rows = shape["upd_rows"]
    device = me[0]
    frontal, right = rest[-2:]
    frontal[:p_size, :] = h[...]
    if upd_rows:
        frontal[p_size:, :] = jnp.zeros_like(frontal[p_size:, :])
    step = min(child_rows, B)
    for piece, piece_masks in zip(pieces, masks, strict=True):
        for part, mask in enumerate(piece_masks):
            source = jnp.bitwise_xor(device, mask)
            if span:
                leaf = source // front
                row_of_map = shape["map_offset"] + leaf // span
                offset = (lax.rem(leaf, span) * front + lax.rem(source, front)) * child_rows
            else:
                row_of_map, offset = source, 0
            for at in range(0, child_rows, step):
                row = offset + at
                target = maps[row_of_map, row // B] * B + lax.rem(row, B)
                where = pl.ds(pl.multiple_of(target, 8), step)
                here = part * child_rows + at
                frontal[where, :] += piece[here : here + step, :]
    right[...] = wide(frontal[:p_size, :])
    z = product(tall(factor[...]), right[...])
    if shape["earlier"]:
        at = 0
        for array in earlier:
            rest[0][at : at + array.shape[0], :] = array[...]
            at += array.shape[0]
        rest[0][at : at + z.shape[0], :] = z
    else:
        rest[0][...] = z
    if upd_rows:
        group_mask = shape["group"] - 1
        rank = jnp.bitwise_and(device, group_mask)
        rest[1][...] = frontal[pl.ds(pl.multiple_of(p_size + rank * upd_rows, 8), upd_rows), :]


def solve_pivots(me, maps, pieces, h, factor, block, earlier, **shape):
    rows = block[1]
    columns = h.shape[1]
    p_size = h.shape[0]
    upd_rows = shape["upd_rows"]
    shape |= {"p_size": p_size, "earlier": len(earlier)}
    total = rows + sum(array.shape[0] for array in earlier)
    outs = [jax.ShapeDtypeStruct((total, columns), F32)]
    if upd_rows:
        outs.append(jax.ShapeDtypeStruct((upd_rows, columns), F32))
    frontal_rows = p_size + upd_rows * shape["group"]
    return pl.pallas_call(
        functools.partial(pivot_kernel, [masks for _, masks in pieces], shape),
        grid=(1,),
        out_shape=tuple(outs),
        in_specs=[SMEM, SMEM]
        + [VMEM] * (len(pieces) + 1)
        + [pl.BlockSpec((rows, p_size), lambda i: (block[0], 0))]
        + [VMEM] * len(earlier),
        out_specs=tuple(VMEM for _ in outs),
        scratch_shapes=[
            pltpu.VMEM((frontal_rows, columns), F32),
            pltpu.VMEM((p_size, 2 * columns), BF16),
        ],
        compiler_params=pltpu.CompilerParams(vmem_limit_bytes=40 * MIB),
        cost_estimate=pl.CostEstimate(
            flops=2 * rows * p_size * columns * 3, bytes_accessed=8 * 10**6, transcendentals=0
        ),
        name="pivots",
    )(me, maps, *[array for array, _ in pieces], h, factor, *earlier)


def update_kernel(masks, group, me, *refs):
    count = len(masks)
    pieces = refs[:count]
    side, factor, w, right = refs[count:]
    rank = jnp.bitwise_and(me[0], group - 1)
    for piece, piece_masks in zip(pieces, masks, strict=True):
        rows = piece.shape[0] // len(piece_masks)
        for part, mask in enumerate(piece_masks):
            source = jnp.bitwise_xor(rank, mask)
            where = pl.ds(pl.multiple_of(source * rows, 16), rows)
            right[where, :] = wide(piece[part * rows : (part + 1) * rows, :])
    w[...] = side[...] - product(tall(factor[...]), right[...])


def solve_update(me, pieces, side, factor, block, group):
    rows = block[1]
    columns = side.shape[1]
    p_size = factor.shape[1]
    return pl.pallas_call(
        functools.partial(update_kernel, [masks for _, masks in pieces], group),
        grid=(1,),
        out_shape=jax.ShapeDtypeStruct((rows, columns), F32),
        in_specs=[SMEM]
        + [VMEM] * (len(pieces) + 1)
        + [pl.BlockSpec((rows, p_size), lambda i: (block[0], 0))],
        out_specs=VMEM,
        scratch_shapes=[pltpu.VMEM((p_size, 2 * columns), BF16)],
        compiler_params=pltpu.CompilerParams(vmem_limit_bytes=40 * MIB),
        cost_estimate=pl.CostEstimate(
            flops=2 * rows * p_size * columns * 3, bytes_accessed=8 * 10**6, transcendentals=0
        ),
        name="update",
    )(me, *[array for array, _ in pieces], side, factor)


def per_device(
    sub_rhs,
    sub_dinv,
    sub_off,
    sub_pattern,
    sub_update,
    sub_map,
    front_rhs,
    piv_inverse,
    upd_factor,
    front_map,
):
    front_size = lax.axis_size("front")
    leaf_size = lax.axis_size("leaf")
    level_count = leaf_size.bit_length()
    p_size = piv_inverse.shape[1]
    u_size = upd_factor.shape[0] * front_size * leaf_size // (2 * (leaf_size - 1))
    me = (lax.axis_index("leaf") * front_size + lax.axis_index("front")).reshape(1)

    known = []
    offset = 0
    for level in range(1, level_count + 1):
        group = front_size * 2 ** (level - 1)
        rows = p_size // group
        mine = front_rhs[offset : offset + rows]
        groups = [
            list(range(first, first + group))
            for first in range(0, front_size * leaf_size, group)
        ]
        known.append(lax.all_gather(mine, AXES, axis=0, tiled=True, axis_index_groups=groups))
        offset += rows

    flat, update = solve_subtree(sub_rhs, sub_dinv, sub_off, sub_pattern, sub_update)
    pieces = spread(update, front_size)
    maps, map_offset, child_span = sub_map, 0, 0
    earlier = []
    for level in range(1, level_count + 1):
        group = front_size * 2 ** (level - 1)
        rows = p_size // group
        last = level == level_count
        out = solve_pivots(
            me,
            maps,
            pieces,
            known[level - 1],
            piv_inverse,
            (2**level - 2, rows),
            earlier if last else [],
            front=front_size,
            child_rows=update.shape[0],
            child_span=child_span,
            map_offset=map_offset,
            upd_rows=0 if last else u_size // group,
            group=group,
        )
        if last:
            return flat, out[0]
        z, side = out
        earlier.append(z)
        z_pieces = spread(z, group)
        update = solve_update(me, z_pieces, side, upd_factor, (2**level - 2, u_size // group), group)
        pieces = spread(update, 2 * group)
        map_offset = 0 if level == 1 else map_offset + leaf_size // child_span
        child_span = 2 ** (level - 1)
        maps = front_map


def solution(mesh):
    split = P(AXES)
    return jax.shard_map(
        per_device,
        mesh=mesh,
        in_specs=(split, split, split, split, split, P(), split, split, split, P()),
        out_specs=(split, split),
        check_vma=False,
    )
```

```python
import functools

import jax
import jax.numpy as jnp
from jax import lax
from jax.experimental import pallas as pl
from jax.experimental.pallas import tpu as pltpu
from jax.sharding import PartitionSpec as P

AXES = ("leaf", "front")
B = 128
BF16 = jnp.bfloat16
F32 = jnp.float32
ANY = pl.BlockSpec(memory_space=pl.ANY)
VMEM = pl.BlockSpec(memory_space=pltpu.VMEM)
HBM = pl.BlockSpec(memory_space=pltpu.HBM)
SMEM = pl.BlockSpec(memory_space=pltpu.SMEM)
MIB = 2**20


def in_hbm(x):
    return pltpu.with_memory_space_constraint(x, pltpu.HBM)


def in_vmem(x):
    return pltpu.with_memory_space_constraint(x, pltpu.VMEM)


def halves(x):
    high = x.astype(BF16)
    return high, (x - high.astype(F32)).astype(BF16)


def tall(x):
    return jnp.concatenate(halves(x), 0)


def wide(x):
    return jnp.concatenate(halves(x), 1)


def product(left, right):
    both = jnp.dot(left, right, preferred_element_type=F32)
    rows, cols = left.shape[0] // 2, right.shape[1] // 2
    return both[:rows, :cols] + both[:rows, cols:] + both[rows:, :cols]


def subtree_kernel(
    bounds, pattern_in, rhs_in, dinv_in, off_in, upd_in, y_out, w, *scratch
):
    pattern, rhs, dinv, off, upd, y, coef, lead, solved, sems, end_sems = scratch
    rounds = len(bounds) - 1

    def loads(r):
        low, high = bounds[r : r + 2]
        above = max(low - 1, 0)
        return [
            pltpu.make_async_copy(dinv_in.at[low:high], dinv.at[low:high], sems.at[r, 0]),
            pltpu.make_async_copy(
                rhs_in.at[low * B : high * B], rhs.at[low * B : high * B], sems.at[r, 1]
            ),
            pltpu.make_async_copy(
                off_in.at[above : high - 1], off.at[above : high - 1], sems.at[r, 2]
            ),
        ]

    def store(r):
        rows = slice(bounds[r] * B, bounds[r + 1] * B)
        return pltpu.make_async_copy(y.at[rows], y_out.at[rows], sems.at[r, 3])

    pattern_copy = pltpu.make_async_copy(pattern_in, pattern, end_sems.at[0])
    upd_copy = pltpu.make_async_copy(upd_in, upd, end_sems.at[1])
    pattern_copy.start()
    for r in range(rounds):
        for copy in loads(r):
            copy.start()
    upd_copy.start()

    def put(i, value):
        rows = slice(i * B, (i + 1) * B)
        y[rows, :] = value
        solved[rows, :] = wide(value)

    def prepare(i):
        right = jnp.concatenate([off[i - 1, 0], off[i - 1, 1], rhs[i * B : (i + 1) * B, :]], 1)
        out = product(tall(dinv[i]), wide(right))
        lead[i] = out[:, 2 * B :]
        coef[i] = tall(-out[:, : 2 * B])

    def step(i):
        first = pl.multiple_of(pattern[0, i - 1] * B, B)
        second = pl.multiple_of(pattern[1, i - 1] * B, B)
        known = jnp.concatenate([solved[pl.ds(first, B), :], solved[pl.ds(second, B), :]], 0)
        put(i, lead[i] + product(coef[i], known))

    pattern_copy.wait()
    for r in range(rounds):
        for copy in loads(r):
            copy.wait()
        if r == 0:
            put(0, product(tall(dinv[0]), wide(rhs[:B, :])))
        low, high = max(bounds[r], 1), bounds[r + 1]
        prepare(low)
        for i in range(low, high):
            if i + 1 < high:
                prepare(i + 1)
            step(i)
        store(r).start()
    upd_copy.wait()
    w[...] = -product(tall(upd[...]), solved[...])
    for r in range(rounds):
        store(r).wait()


def solve_subtree(rhs, dinv, off, pattern, upd):
    count = dinv.shape[0]
    bounds = [0, count // 6, count // 2, count]
    return pl.pallas_call(
        functools.partial(subtree_kernel, bounds),
        out_shape=(
            jax.ShapeDtypeStruct(rhs.shape, F32),
            jax.ShapeDtypeStruct((upd.shape[0], rhs.shape[1]), F32),
        ),
        in_specs=[HBM] * 5,
        out_specs=(HBM, VMEM),
        scratch_shapes=[
            pltpu.SMEM(pattern.shape, jnp.int32),
            pltpu.VMEM(rhs.shape, F32),
            pltpu.VMEM(dinv.shape, F32),
            pltpu.VMEM(off.shape, F32),
            pltpu.VMEM(upd.shape, F32),
            pltpu.VMEM(rhs.shape, F32),
            pltpu.VMEM((count, 2 * B, 2 * B), BF16),
            pltpu.VMEM((count, B, B), F32),
            pltpu.VMEM((count * B, 2 * B), BF16),
            pltpu.SemaphoreType.DMA((len(bounds) - 1, 4)),
            pltpu.SemaphoreType.DMA((2,)),
        ],
        compiler_params=pltpu.CompilerParams(vmem_limit_bytes=32 * MIB),
        cost_estimate=pl.CostEstimate(flops=10**6, bytes_accessed=10**5, transcendentals=0),
        name="subtree",
    )(*[in_hbm(x) for x in (pattern, rhs, dinv, off, upd)])


def exchange(x, mask):
    size = lax.axis_size("leaf") * lax.axis_size("front")
    return lax.ppermute(x, AXES, [(source, source ^ mask) for source in range(size)])


def spread(x, group, through=lambda x: x):
    masks = [0]
    apart = group // 2
    while apart >= 16:
        far = exchange(x, apart)
        x = through(x)
        x = jnp.concatenate([x, far], 0)
        masks = masks + [mask ^ apart for mask in masks]
        apart //= 2
        through = lambda value: value
    low = 2 * apart
    arrays = [(mask, exchange(x, mask)) for mask in range(low - 2, 0, -2)]
    if low > 4:
        arrays[0] = (low - 2, through(arrays[0][1]))
        arrays.append((0, x))
    else:
        arrays.append((0, through(x)))
    arrays += [(mask ^ 1, exchange(array, 1)) for mask, array in arrays]
    return [(array, [mask ^ high for high in masks]) for mask, array in arrays]


def factor_kernel(block, factor, own, out, own_out, held, sems):
    rows = held.shape[0]
    first, step = block[0] * block[1], held.shape[0] // sems.shape[0]
    loads = [
        pltpu.make_async_copy(
            factor.at[first + at : first + at + step], held.at[at : at + step], sems.at[at // step]
        )
        for at in range(0, rows, step)
    ]
    for load in loads:
        load.start()
    own_out[...] = own[...]
    for n, load in enumerate(loads):
        load.wait()
        high, low = halves(held[n * step : (n + 1) * step, :])
        out[n * step : (n + 1) * step, :] = high
        out[rows + n * step : rows + (n + 1) * step, :] = low


def prepare_factor(factor, block, own):
    rows, columns = block[1], factor.shape[1]
    return pl.pallas_call(
        functools.partial(factor_kernel, block),
        out_shape=(
            jax.ShapeDtypeStruct((2 * rows, columns), BF16),
            jax.ShapeDtypeStruct(own.shape, F32),
        ),
        in_specs=[HBM, VMEM],
        out_specs=(VMEM, VMEM),
        scratch_shapes=[
            pltpu.VMEM((rows, columns), F32),
            pltpu.SemaphoreType.DMA((max(1, min(4, rows // 16)),)),
        ],
        compiler_params=pltpu.CompilerParams(vmem_limit_bytes=16 * MIB),
        cost_estimate=pl.CostEstimate(
            flops=0, bytes_accessed=8 * rows * columns, transcendentals=0
        ),
        name="factor",
    )(in_hbm(factor), own)


def pivot_kernel(masks, shape, me, maps, *refs):
    count = len(masks)
    pieces, refs = refs[:count], refs[count:]
    own_h, refs = refs[: shape["h_count"]], refs[shape["h_count"] :]
    factor, refs = refs[0], refs[1:]
    earlier, rest = refs[: shape["earlier"]], refs[shape["earlier"] :]
    front = shape["front"]
    p_size, child_rows, span = shape["p_size"], shape["child_rows"], shape["child_span"]
    upd_rows = shape["upd_rows"]
    device = me[0]
    frontal, right = rest[-2:]
    h_rows = p_size // shape["group"]
    for n, start, mask in shape["h_parts"]:
        rank = jnp.bitwise_and(jnp.bitwise_xor(device, mask), shape["group"] - 1)
        row = rank * h_rows
        part = own_h[n][start : start + h_rows, :]
        if h_rows >= B:
            frontal[pl.ds(row // B, h_rows // B)] = part.reshape(h_rows // B, B, -1)
        else:
            inner = pl.multiple_of(lax.rem(row, B), h_rows)
            frontal[row // B, pl.ds(inner, h_rows), :] = part
    if upd_rows:
        frontal[p_size // B :, :, :] = jnp.zeros_like(frontal[p_size // B :, :, :])
    if shape["earlier"]:
        done = 0
        for array in earlier:
            rest[0][done : done + array.shape[0], :] = array[...]
            done += array.shape[0]
    step = min(child_rows, B)
    for piece, piece_masks in zip(pieces, masks, strict=True):
        for part, mask in enumerate(piece_masks):
            source = jnp.bitwise_xor(device, mask)
            if span:
                leaf = source // front
                row_of_map = shape["map_offset"] + leaf // span
                offset = (lax.rem(leaf, span) * front + lax.rem(source, front)) * child_rows
            else:
                row_of_map, offset = source, 0
            for at in range(0, child_rows, step):
                row = offset + at
                target = maps[row // B, row_of_map]
                inner = pl.multiple_of(lax.rem(row, B), step)
                here = part * child_rows + at
                if step == B:
                    frontal[target] += piece[here : here + step, :]
                else:
                    frontal[target, pl.ds(inner, step), :] += piece[here : here + step, :]
    right[...] = wide(frontal[: p_size // B].reshape(p_size, -1))
    z = product(factor[...], right[...])
    if shape["earlier"]:
        rest[0][done : done + z.shape[0], :] = z
    else:
        rest[0][...] = z
    if upd_rows:
        rank = jnp.bitwise_and(device, shape["group"] - 1)
        row = rank * upd_rows
        if upd_rows >= B:
            side = frontal[pl.ds(p_size // B + row // B, upd_rows // B)]
            rest[1][...] = side.reshape(upd_rows, -1)
        else:
            inner = pl.multiple_of(lax.rem(row, B), upd_rows)
            rest[1][...] = frontal[p_size // B + row // B, pl.ds(inner, upd_rows), :]


def solve_pivots(me, maps, pieces, h, factor, earlier, **shape):
    rows = factor.shape[0] // 2
    columns = pieces[0][0].shape[1]
    p_size = factor.shape[1]
    upd_rows = shape["upd_rows"]
    shape |= {
        "p_size": p_size,
        "earlier": len(earlier),
        "h_count": len(h[0]),
        "h_parts": h[1],
    }
    total = rows + sum(array.shape[0] for array in earlier)
    outs = [jax.ShapeDtypeStruct((total, columns), F32)]
    if upd_rows:
        outs.append(jax.ShapeDtypeStruct((upd_rows, columns), F32))
    frontal_rows = p_size + upd_rows * shape["group"]
    operands = [array for array, _ in pieces] + h[0] + [factor, *earlier]
    return pl.pallas_call(
        functools.partial(pivot_kernel, [masks for _, masks in pieces], shape),
        out_shape=tuple(outs),
        in_specs=[SMEM, SMEM] + [VMEM] * len(operands),
        out_specs=tuple(VMEM for _ in outs),
        scratch_shapes=[
            pltpu.VMEM((frontal_rows // B, B, columns), F32),
            pltpu.VMEM((p_size, 2 * columns), BF16),
        ],
        compiler_params=pltpu.CompilerParams(vmem_limit_bytes=24 * MIB),
        cost_estimate=pl.CostEstimate(
            flops=2 * rows * p_size * columns * 3, bytes_accessed=8 * 10**6, transcendentals=0
        ),
        name="pivots",
    )(me, maps, *operands)


def update_kernel(masks, group, me, *refs):
    count = len(masks)
    pieces = refs[:count]
    side, factor, w, right = refs[count:]
    rank = jnp.bitwise_and(me[0], group - 1)
    for piece, piece_masks in zip(pieces, masks, strict=True):
        rows = piece.shape[0] // len(piece_masks)
        for part, mask in enumerate(piece_masks):
            source = jnp.bitwise_xor(rank, mask)
            where = pl.ds(pl.multiple_of(source * rows, 16), rows)
            right[where, :] = wide(piece[part * rows : (part + 1) * rows, :])
    w[...] = side[...] - product(factor[...], right[...])


def solve_update(me, pieces, side, factor, group):
    rows, columns = side.shape
    p_size = factor.shape[1]
    return pl.pallas_call(
        functools.partial(update_kernel, [masks for _, masks in pieces], group),
        out_shape=jax.ShapeDtypeStruct((rows, columns), F32),
        in_specs=[SMEM] + [VMEM] * (len(pieces) + 2),
        out_specs=VMEM,
        scratch_shapes=[pltpu.VMEM((p_size, 2 * columns), BF16)],
        compiler_params=pltpu.CompilerParams(vmem_limit_bytes=24 * MIB),
        cost_estimate=pl.CostEstimate(
            flops=2 * rows * p_size * columns * 3, bytes_accessed=8 * 10**6, transcendentals=0
        ),
        name="update",
    )(me, *[array for array, _ in pieces], side, factor)


def join_kernel(plans, after, *refs):
    del after
    outs = refs[len(refs) - len(plans) :]
    for out, parts in zip(outs, plans, strict=True):
        at = 0
        for n, start, stop in parts:
            out[at : at + stop - start, :] = refs[n][start:stop, :]
            at += stop - start


def join_rows(after, arrays, plans):
    totals = [sum(stop - start for _, start, stop in parts) for parts in plans]
    return pl.pallas_call(
        functools.partial(join_kernel, plans),
        out_shape=tuple(
            jax.ShapeDtypeStruct((total, arrays[0].shape[1]), F32) for total in totals
        ),
        in_specs=[ANY] + [VMEM] * len(arrays),
        out_specs=tuple(VMEM for _ in totals),
        compiler_params=pltpu.CompilerParams(vmem_limit_bytes=8 * MIB),
        cost_estimate=pl.CostEstimate(flops=0, bytes_accessed=10**6, transcendentals=0),
        name="join",
    )(after, *arrays)


class Rhs:
    def __init__(self, front_rhs, p_size, groups):
        self.rows = [p_size // group for group in groups]
        self.total = front_rhs.shape[0]
        self.masks = [0, 2]
        self.held = [front_rhs, exchange(front_rhs, 2)]
        self.level = 0

    def next_level(self, after):
        rows, group = self.rows[self.level], 2 * len(self.masks)
        span = sum(self.rows[self.level :])
        parts = [
            (n, at * span) for n, array in enumerate(self.held) for at in range(array.shape[0] // span)
        ]
        plans = [[(n, at, at + rows) for n, at in parts]]
        last = self.level + 1 == len(self.rows)
        if not last:
            plans.append([(n, at + rows, at + span) for n, at in parts])
        mine, *rest = join_rows(after, self.held, plans)
        other = exchange(mine, 1)
        place = [(0, at * rows, mask) for at, mask in enumerate(self.masks)]
        place += [(1, at * rows, mask ^ 1) for at, mask in enumerate(self.masks)]
        if not last:
            self.held = [rest[0], exchange(rest[0], group)]
            self.masks = self.masks + [mask ^ group for mask in self.masks]
        self.level += 1
        return [mine, other], place


def per_device(
    sub_rhs,
    sub_dinv,
    sub_off,
    sub_pattern,
    sub_update,
    sub_map,
    front_rhs,
    piv_inverse,
    upd_factor,
    front_map,
):
    front_size = lax.axis_size("front")
    leaf_size = lax.axis_size("leaf")
    level_count = leaf_size.bit_length()
    p_size = piv_inverse.shape[1]
    u_size = upd_factor.shape[0] * front_size * leaf_size // (2 * (leaf_size - 1))
    me = (lax.axis_index("leaf") * front_size + lax.axis_index("front")).reshape(1)

    size = front_size * leaf_size
    groups = [front_size * 2**level for level in range(level_count)]
    columns = sub_rhs.shape[1]
    sizes = [p_size // group for group in groups]
    rhs = Rhs(front_rhs, p_size, groups)

    flat, update = solve_subtree(sub_rhs, sub_dinv, sub_off, sub_pattern.T, sub_update)
    kept = []

    def keep(factor, block):
        def through(x):
            factor_rows, x = prepare_factor(factor, block, x)
            kept[:] = [factor_rows]
            return x

        return through

    pieces = spread(update, front_size, keep(piv_inverse, (0, sizes[0])))
    factor = kept[0]
    h = [rhs.next_level(update)]
    maps, map_offset, child_span = sub_map.T, 0, 0
    earlier = []
    for level in range(1, level_count + 1):
        group = groups[level - 1]
        last = level == level_count
        out = solve_pivots(
            me,
            maps,
            pieces,
            h[level - 1],
            factor,
            earlier if last else [],
            front=front_size,
            child_rows=update.shape[0],
            child_span=child_span,
            map_offset=map_offset,
            upd_rows=0 if last else u_size // group,
            group=group,
        )
        if last:
            return flat, out[0]
        z, side = out
        earlier.append(z)
        if len(h) < level_count:
            h.append(rhs.next_level(z))
        z_pieces = spread(z, group, keep(upd_factor, (2**level - 2, u_size // group)))
        update = solve_update(me, z_pieces, side, kept[0], group)
        pieces = spread(update, 2 * group, keep(piv_inverse, (2 ** (level + 1) - 2, sizes[level])))
        factor = kept[0]
        if len(h) < level_count:
            h.append(rhs.next_level(update))
        map_offset = 0 if level == 1 else map_offset + leaf_size // child_span
        child_span = 2 ** (level - 1)
        maps = front_map.T


def solution(mesh):
    split = P(AXES)
    return jax.shard_map(
        per_device,
        mesh=mesh,
        in_specs=(split, split, split, split, split, P(), split, split, split, P()),
        out_specs=(split, split),
        check_vma=False,
    )
```

```python
import functools

import jax
import jax.numpy as jnp
from jax import lax
from jax.experimental import pallas as pl
from jax.experimental.pallas import tpu as pltpu
from jax.sharding import PartitionSpec as P

AXES = ("leaf", "front")
B = 128
BF16 = jnp.bfloat16
F32 = jnp.float32
ANY = pl.BlockSpec(memory_space=pl.ANY)
VMEM = pl.BlockSpec(memory_space=pltpu.VMEM)
HBM = pl.BlockSpec(memory_space=pltpu.HBM)
SMEM = pl.BlockSpec(memory_space=pltpu.SMEM)
MIB = 2**20


def in_hbm(x):
    return pltpu.with_memory_space_constraint(x, pltpu.HBM)


def in_vmem(x):
    return pltpu.with_memory_space_constraint(x, pltpu.VMEM)


def halves(x):
    high = x.astype(BF16)
    return high, (x - high.astype(F32)).astype(BF16)


def tall(x):
    return jnp.concatenate(halves(x), 0)


def wide(x):
    return jnp.concatenate(halves(x), 1)


def product(left, right):
    both = jnp.dot(left, right, preferred_element_type=F32)
    rows, cols = left.shape[0] // 2, right.shape[1] // 2
    return both[:rows, :cols] + both[:rows, cols:] + both[rows:, :cols]


def subtree_kernel(
    bounds, pattern_in, rhs_in, dinv_in, off_in, upd_in, y_out, w, *scratch
):
    pattern, rhs, dinv, off, upd, y, coef, lead, solved, sems, end_sems = scratch
    rounds = len(bounds) - 1

    def loads(r):
        low, high = bounds[r : r + 2]
        above = max(low - 1, 0)
        return [
            pltpu.make_async_copy(dinv_in.at[low:high], dinv.at[low:high], sems.at[r, 0]),
            pltpu.make_async_copy(
                rhs_in.at[low * B : high * B], rhs.at[low * B : high * B], sems.at[r, 1]
            ),
            pltpu.make_async_copy(
                off_in.at[above : high - 1], off.at[above : high - 1], sems.at[r, 2]
            ),
        ]

    def store(r):
        rows = slice(bounds[r] * B, bounds[r + 1] * B)
        return pltpu.make_async_copy(y.at[rows], y_out.at[rows], sems.at[r, 3])

    pattern_copy = pltpu.make_async_copy(pattern_in, pattern, end_sems.at[0])
    upd_copy = pltpu.make_async_copy(upd_in, upd, end_sems.at[1])
    pattern_copy.start()
    for r in range(rounds):
        for copy in loads(r):
            copy.start()
    upd_copy.start()

    def put(i, value):
        rows = slice(i * B, (i + 1) * B)
        y[rows, :] = value
        solved[rows, :] = wide(value)

    def prepare(i):
        right = jnp.concatenate([off[i - 1, 0], off[i - 1, 1], rhs[i * B : (i + 1) * B, :]], 1)
        out = product(tall(dinv[i]), wide(right))
        lead[i] = out[:, 2 * B :]
        coef[i] = tall(-out[:, : 2 * B])

    def step(i):
        first = pl.multiple_of(pattern[0, i - 1] * B, B)
        second = pl.multiple_of(pattern[1, i - 1] * B, B)
        known = jnp.concatenate([solved[pl.ds(first, B), :], solved[pl.ds(second, B), :]], 0)
        put(i, lead[i] + product(coef[i], known))

    pattern_copy.wait()
    for r in range(rounds):
        for copy in loads(r):
            copy.wait()
        if r == 0:
            put(0, product(tall(dinv[0]), wide(rhs[:B, :])))
        low, high = max(bounds[r], 1), bounds[r + 1]
        prepare(low)
        for i in range(low, high):
            if i + 1 < high:
                prepare(i + 1)
            step(i)
        store(r).start()
    upd_copy.wait()
    w[...] = -product(tall(upd[...]), solved[...])
    for r in range(rounds):
        store(r).wait()


def solve_subtree(rhs, dinv, off, pattern, upd):
    count = dinv.shape[0]
    bounds = [0, count // 6, count // 2, count]
    return pl.pallas_call(
        functools.partial(subtree_kernel, bounds),
        out_shape=(
            jax.ShapeDtypeStruct(rhs.shape, F32),
            jax.ShapeDtypeStruct((upd.shape[0], rhs.shape[1]), F32),
        ),
        in_specs=[HBM] * 5,
        out_specs=(HBM, VMEM),
        scratch_shapes=[
            pltpu.SMEM(pattern.shape, jnp.int32),
            pltpu.VMEM(rhs.shape, F32),
            pltpu.VMEM(dinv.shape, F32),
            pltpu.VMEM(off.shape, F32),
            pltpu.VMEM(upd.shape, F32),
            pltpu.VMEM(rhs.shape, F32),
            pltpu.VMEM((count, 2 * B, 2 * B), BF16),
            pltpu.VMEM((count, B, B), F32),
            pltpu.VMEM((count * B, 2 * B), BF16),
            pltpu.SemaphoreType.DMA((len(bounds) - 1, 4)),
            pltpu.SemaphoreType.DMA((2,)),
        ],
        compiler_params=pltpu.CompilerParams(vmem_limit_bytes=32 * MIB),
        cost_estimate=pl.CostEstimate(flops=10**6, bytes_accessed=10**5, transcendentals=0),
        name="subtree",
    )(*[in_hbm(x) for x in (pattern, rhs, dinv, off, upd)])


def exchange(x, mask):
    size = lax.axis_size("leaf") * lax.axis_size("front")
    return lax.ppermute(x, AXES, [(source, source ^ mask) for source in range(size)])


def spread(x, group, *throughs):
    masks = [0]
    apart = group // 2
    while apart >= 16:
        x = jnp.concatenate([x, exchange(x, apart)], 0)
        masks = masks + [mask ^ apart for mask in masks]
        apart //= 2
    low = 2 * apart
    arrays = [(mask, exchange(x, mask)) for mask in range(low - 2, 0, -2)]
    if low > 4:
        for n, through in enumerate(throughs):
            arrays[n] = (arrays[n][0], through(arrays[n][1]))
        arrays.append((0, x))
    else:
        arrays.append((0, throughs[0](x)))
    arrays += [(mask ^ 1, exchange(array, 1)) for mask, array in arrays]
    return [(array, [mask ^ high for high in masks]) for mask, array in arrays]


def factor_kernel(block, factor, own, out, own_out, held, sems):
    rows = held.shape[0]
    first, step = block[0] * block[1], held.shape[0] // sems.shape[0]
    loads = [
        pltpu.make_async_copy(
            factor.at[first + at : first + at + step], held.at[at : at + step], sems.at[at // step]
        )
        for at in range(0, rows, step)
    ]
    for load in loads:
        load.start()
    own_out[...] = own[...]
    for n, load in enumerate(loads):
        load.wait()
        high, low = halves(held[n * step : (n + 1) * step, :])
        out[n * step : (n + 1) * step, :] = high
        out[rows + n * step : rows + (n + 1) * step, :] = low


def prepare_factor(factor, block, own):
    rows, columns = block[1], factor.shape[1]
    return pl.pallas_call(
        functools.partial(factor_kernel, block),
        out_shape=(
            jax.ShapeDtypeStruct((2 * rows, columns), BF16),
            jax.ShapeDtypeStruct(own.shape, F32),
        ),
        in_specs=[HBM, VMEM],
        out_specs=(VMEM, VMEM),
        scratch_shapes=[
            pltpu.VMEM((rows, columns), F32),
            pltpu.SemaphoreType.DMA((max(1, min(4, rows // 16)),)),
        ],
        compiler_params=pltpu.CompilerParams(vmem_limit_bytes=16 * MIB),
        cost_estimate=pl.CostEstimate(
            flops=0, bytes_accessed=8 * rows * columns, transcendentals=0
        ),
        name="factor",
    )(in_hbm(factor), own)


def pivot_kernel(masks, shape, me, maps, *refs):
    count = len(masks)
    pieces, refs = refs[:count], refs[count:]
    own_h, refs = refs[: shape["h_count"]], refs[shape["h_count"] :]
    factor, refs = refs[0], refs[1:]
    earlier, refs = refs[: shape["earlier"]], refs[shape["earlier"] :]
    rides, rest = refs[: shape["rides"]], refs[shape["rides"] + shape["ahead"] :]
    front = shape["front"]
    p_size, child_rows, span = shape["p_size"], shape["child_rows"], shape["child_span"]
    upd_rows = shape["upd_rows"]
    device = me[0]
    frontal, right = rest[-2:]
    h_rows = p_size // shape["group"]
    for n, start, mask in shape["h_parts"]:
        rank = jnp.bitwise_and(jnp.bitwise_xor(device, mask), shape["group"] - 1)
        row = rank * h_rows
        part = own_h[n][start : start + h_rows, :]
        if h_rows >= B:
            frontal[pl.ds(row // B, h_rows // B)] = part.reshape(h_rows // B, B, -1)
        else:
            inner = pl.multiple_of(lax.rem(row, B), h_rows)
            frontal[row // B, pl.ds(inner, h_rows), :] = part
    if upd_rows:
        frontal[p_size // B :, :, :] = jnp.zeros_like(frontal[p_size // B :, :, :])
    if shape["earlier"]:
        done = 0
        for n, array in enumerate(earlier):
            rows = p_size // (front * 2**n)
            rest[0][done : done + rows, :] = array[:rows, :]
            done += rows
    step = min(child_rows, B)
    for piece, piece_masks in zip(pieces, masks, strict=True):
        for part, mask in enumerate(piece_masks):
            source = jnp.bitwise_xor(device, mask)
            if span:
                leaf = source // front
                row_of_map = shape["map_offset"] + leaf // span
                offset = (lax.rem(leaf, span) * front + lax.rem(source, front)) * child_rows
            else:
                row_of_map, offset = source, 0
            for at in range(0, child_rows, step):
                row = offset + at
                target = maps[row // B, row_of_map]
                inner = pl.multiple_of(lax.rem(row, B), step)
                here = part * child_rows + at
                if step == B:
                    frontal[target] += piece[here : here + step, :]
                else:
                    frontal[target, pl.ds(inner, step), :] += piece[here : here + step, :]
    right[...] = wide(frontal[: p_size // B].reshape(p_size, -1))
    z = product(factor[...], right[...])
    if shape["rides"]:
        rest[0][: z.shape[0], :] = z
        rest[0][z.shape[0] :, :] = rides[0][...]
    elif shape["earlier"]:
        rest[0][done : done + z.shape[0], :] = z
    else:
        rest[0][...] = z
    if upd_rows:
        rank = jnp.bitwise_and(device, shape["group"] - 1)
        row = rank * upd_rows
        if upd_rows >= B:
            side = frontal[pl.ds(p_size // B + row // B, upd_rows // B)]
            rest[1][...] = side.reshape(upd_rows, -1)
        else:
            inner = pl.multiple_of(lax.rem(row, B), upd_rows)
            rest[1][...] = frontal[p_size // B + row // B, pl.ds(inner, upd_rows), :]


def solve_pivots(me, maps, pieces, h, factor, earlier, rides, ahead, **shape):
    rows = factor.shape[0] // 2
    columns = pieces[0][0].shape[1]
    p_size = factor.shape[1]
    upd_rows = shape["upd_rows"]
    shape |= {
        "p_size": p_size,
        "earlier": len(earlier),
        "rides": len(rides),
        "ahead": len(ahead),
        "h_count": len(h[0]),
        "h_parts": h[1],
    }
    total = sum(p_size // (shape["front"] * 2**n) for n in range(len(earlier)))
    total += rows + sum(array.shape[0] for array in rides)
    outs = [jax.ShapeDtypeStruct((total, columns), F32)]
    if upd_rows:
        outs.append(jax.ShapeDtypeStruct((upd_rows, columns), F32))
    frontal_rows = p_size + upd_rows * shape["group"]
    operands = [array for array, _ in pieces] + h[0] + [factor, *earlier, *rides, *ahead]
    return pl.pallas_call(
        functools.partial(pivot_kernel, [masks for _, masks in pieces], shape),
        out_shape=tuple(outs),
        in_specs=[SMEM, SMEM] + [VMEM] * (len(operands) - len(ahead)) + [ANY] * len(ahead),
        out_specs=tuple(VMEM for _ in outs),
        scratch_shapes=[
            pltpu.VMEM((frontal_rows // B, B, columns), F32),
            pltpu.VMEM((p_size, 2 * columns), BF16),
        ],
        compiler_params=pltpu.CompilerParams(vmem_limit_bytes=24 * MIB),
        cost_estimate=pl.CostEstimate(
            flops=2 * rows * p_size * columns * 3, bytes_accessed=8 * 10**6, transcendentals=0
        ),
        name="pivots",
    )(me, maps, *operands)


def update_kernel(masks, group, me, *refs):
    count = len(masks)
    pieces = refs[:count]
    side, factor, w, right = refs[count:]
    rank = jnp.bitwise_and(me[0], group - 1)
    used = right.shape[0] // group
    for piece, piece_masks in zip(pieces, masks, strict=True):
        rows = piece.shape[0] // len(piece_masks)
        for part, mask in enumerate(piece_masks):
            source = jnp.bitwise_xor(rank, mask)
            where = pl.ds(pl.multiple_of(source * used, 16), used)
            right[where, :] = wide(piece[part * rows : part * rows + used, :])
    w[...] = side[...] - product(factor[...], right[...])


def solve_update(me, pieces, side, factor, group):
    rows, columns = side.shape
    p_size = factor.shape[1]
    return pl.pallas_call(
        functools.partial(update_kernel, [masks for _, masks in pieces], group),
        out_shape=jax.ShapeDtypeStruct((rows, columns), F32),
        in_specs=[SMEM] + [VMEM] * (len(pieces) + 2),
        out_specs=VMEM,
        scratch_shapes=[pltpu.VMEM((p_size, 2 * columns), BF16)],
        compiler_params=pltpu.CompilerParams(vmem_limit_bytes=24 * MIB),
        cost_estimate=pl.CostEstimate(
            flops=2 * rows * p_size * columns * 3, bytes_accessed=8 * 10**6, transcendentals=0
        ),
        name="update",
    )(me, *[array for array, _ in pieces], side, factor)


def join_kernel(plans, after, *refs):
    del after
    outs = refs[len(refs) - len(plans) :]
    for out, parts in zip(outs, plans, strict=True):
        at = 0
        for n, start, stop in parts:
            out[at : at + stop - start, :] = refs[n][start:stop, :]
            at += stop - start


def join_rows(after, arrays, plans):
    totals = [sum(stop - start for _, start, stop in parts) for parts in plans]
    return pl.pallas_call(
        functools.partial(join_kernel, plans),
        out_shape=tuple(
            jax.ShapeDtypeStruct((total, arrays[0].shape[1]), F32) for total in totals
        ),
        in_specs=[ANY] + [VMEM] * len(arrays),
        out_specs=tuple(VMEM for _ in totals),
        compiler_params=pltpu.CompilerParams(vmem_limit_bytes=8 * MIB),
        cost_estimate=pl.CostEstimate(flops=0, bytes_accessed=10**6, transcendentals=0),
        name="join",
    )(after, *arrays)


class Rhs:
    def __init__(self, front_rhs, p_size, groups):
        self.rows = [p_size // group for group in groups]
        self.masks = [0, 2]
        self.held = [front_rhs, exchange(front_rhs, 2)]
        self.spans = [front_rhs.shape[0]] * 2
        self.first = 0
        self.done = []
        root = front_rhs[front_rhs.shape[0] - self.rows[-1] :]
        self.root = [root, exchange(root, groups[-1] // 2)]

    def pair_root(self, after):
        plan = [(n, 0, self.rows[-1]) for n in range(2)]
        (self.root_pair,) = join_rows(after, self.root, [plan])

    def next_level(self, after):
        level = len(self.done)
        rows, group = self.rows[level], 2 * len(self.masks)
        rest = sum(self.rows[level + 1 : -1])
        parts = [
            (n, at + self.first)
            for n, (array, span) in enumerate(zip(self.held, self.spans, strict=True))
            for at in range(0, array.shape[0], span)
        ]
        plans = [[(n, at, at + rows) for n, at in parts]]
        if rest:
            plans.append([(n, at + rows, at + rows + rest) for n, at in parts])
        out = join_rows(after, self.held, plans)
        place = [(0, at * rows, mask) for at, mask in enumerate(self.masks)]
        place += [(1, at * rows, mask ^ 1) for at, mask in enumerate(self.masks)]
        self.done.append(([out[0], exchange(out[0], 1)], place))
        if rest:
            self.held = [out[1], exchange(out[1], group)]
            self.spans = [rest, rest]
            self.masks = self.masks + [mask ^ group for mask in self.masks]


def per_device(
    sub_rhs,
    sub_dinv,
    sub_off,
    sub_pattern,
    sub_update,
    sub_map,
    front_rhs,
    piv_inverse,
    upd_factor,
    front_map,
):
    front_size = lax.axis_size("front")
    leaf_size = lax.axis_size("leaf")
    level_count = leaf_size.bit_length()
    p_size = piv_inverse.shape[1]
    u_size = upd_factor.shape[0] * front_size * leaf_size // (2 * (leaf_size - 1))
    me = (lax.axis_index("leaf") * front_size + lax.axis_index("front")).reshape(1)

    size = front_size * leaf_size
    groups = [front_size * 2**level for level in range(level_count)]
    columns = sub_rhs.shape[1]
    sizes = [p_size // group for group in groups]
    rhs = Rhs(front_rhs, p_size, groups)

    flat, update = solve_subtree(sub_rhs, sub_dinv, sub_off, sub_pattern.T, sub_update)
    kept = {}

    def keep(name, factor, block):
        def through(x):
            factor_rows, x = prepare_factor(factor, block, x)
            kept[name] = factor_rows
            return x

        return through

    pieces = spread(update, front_size, keep("pivots", piv_inverse, (0, sizes[0])))
    rhs.next_level(update)
    maps, map_offset, child_span = sub_map.T, 0, 0
    earlier = []
    for level in range(1, level_count + 1):
        group = groups[level - 1]
        last = level == level_count
        out = solve_pivots(
            me,
            maps,
            pieces,
            rhs.done[level - 1],
            kept["pivots"],
            earlier if last else [],
            [rhs.root_pair] if level == level_count - 1 else [],
            [rhs.root_pair] if level == 2 else [],
            front=front_size,
            child_rows=update.shape[0],
            child_span=child_span,
            map_offset=map_offset,
            upd_rows=0 if last else u_size // group,
            group=group,
        )
        if last:
            return flat, out[0]
        z, side = out
        earlier.append(z)
        if level > 1 and len(rhs.done) < level_count - 1:
            rhs.next_level(z)
        throughs = [keep("update", upd_factor, (2**level - 2, u_size // group))]
        following = [keep("pivots", piv_inverse, (2 ** (level + 1) - 2, sizes[level]))]
        if level == level_count - 1:
            throughs, following = throughs + following, []
        z_pieces = spread(z, group, *throughs)
        update = solve_update(me, z_pieces, side, kept["update"], group)
        pieces = spread(update, 2 * group, *following)
        if level == 1:
            rhs.pair_root(update)
        if level == 1:
            rhs.next_level(update)
        if level == level_count - 1:
            parts = []
            for n, (array, masks) in enumerate(z_pieces):
                rows = array.shape[0] // len(masks)
                for at, mask in enumerate(masks):
                    row = at * rows + sizes[level - 1]
                    parts.append((n, row, mask))
                    parts.append((n, row + sizes[level], mask ^ group))
            rhs.done.append(([array for array, _ in z_pieces], parts))
        map_offset = 0 if level == 1 else map_offset + leaf_size // child_span
        child_span = 2 ** (level - 1)
        maps = front_map.T


def solution(mesh):
    split = P(AXES)
    return jax.shard_map(
        per_device,
        mesh=mesh,
        in_specs=(split, split, split, split, split, P(), split, split, split, P()),
        out_specs=(split, split),
        check_vma=False,
    )
```

```python
import functools

import jax
import jax.numpy as jnp
from jax import lax
from jax.experimental import pallas as pl
from jax.experimental.pallas import tpu as pltpu
from jax.sharding import PartitionSpec as P

AXES = ("leaf", "front")
B = 128
BF16 = jnp.bfloat16
F32 = jnp.float32
ANY = pl.BlockSpec(memory_space=pl.ANY)
VMEM = pl.BlockSpec(memory_space=pltpu.VMEM)
HBM = pl.BlockSpec(memory_space=pltpu.HBM)
SMEM = pl.BlockSpec(memory_space=pltpu.SMEM)
MIB = 2**20


def in_hbm(x):
    return pltpu.with_memory_space_constraint(x, pltpu.HBM)


def in_vmem(x):
    return pltpu.with_memory_space_constraint(x, pltpu.VMEM)


def halves(x):
    high = x.astype(BF16)
    return high, (x - high.astype(F32)).astype(BF16)


def tall(x):
    return jnp.concatenate(halves(x), 0)


def wide(x):
    return jnp.concatenate(halves(x), 1)


def product(left, right):
    both = jnp.dot(left, right, preferred_element_type=F32)
    rows, cols = left.shape[0] // 2, right.shape[1] // 2
    return both[:rows, :cols] + both[:rows, cols:] + both[rows:, :cols]


def subtree_kernel(
    bounds, pattern_in, rhs_in, dinv_in, off_in, upd_in, factor_in, y_out, w, factor_out, *scratch
):
    pattern, rhs, dinv, off, upd, y, coef, lead, solved, factor, split, sems, end_sems, split_sems = scratch
    rounds = len(bounds) - 1

    def loads(r):
        low, high = bounds[r : r + 2]
        above = max(low - 1, 0)
        return [
            pltpu.make_async_copy(dinv_in.at[low:high], dinv.at[low:high], sems.at[r, 0]),
            pltpu.make_async_copy(
                rhs_in.at[low * B : high * B], rhs.at[low * B : high * B], sems.at[r, 1]
            ),
            pltpu.make_async_copy(
                off_in.at[above : high - 1], off.at[above : high - 1], sems.at[r, 2]
            ),
        ]

    def store(r):
        rows = slice(bounds[r] * B, bounds[r + 1] * B)
        return pltpu.make_async_copy(y.at[rows], y_out.at[rows], sems.at[r, 3])

    pattern_copy = pltpu.make_async_copy(pattern_in, pattern, end_sems.at[0])
    upd_copy = pltpu.make_async_copy(upd_in, upd, end_sems.at[1])
    factor_copy = pltpu.make_async_copy(
        factor_in.at[: factor.shape[0]], factor, end_sems.at[2]
    )
    pattern_copy.start()
    for r in range(rounds):
        for copy in loads(r):
            copy.start()
    upd_copy.start()
    factor_copy.start()

    def put(i, value):
        rows = slice(i * B, (i + 1) * B)
        y[rows, :] = value
        solved[rows, :] = wide(value)

    def prepare(i):
        right = jnp.concatenate([off[i - 1, 0], off[i - 1, 1], rhs[i * B : (i + 1) * B, :]], 1)
        out = product(tall(dinv[i]), wide(right))
        lead[i] = out[:, 2 * B :]
        coef[i] = tall(-out[:, : 2 * B])

    def step(i):
        first = pl.multiple_of(pattern[0, i - 1] * B, B)
        second = pl.multiple_of(pattern[1, i - 1] * B, B)
        known = jnp.concatenate([solved[pl.ds(first, B), :], solved[pl.ds(second, B), :]], 0)
        put(i, lead[i] + product(coef[i], known))

    count = dinv.shape[0]
    late = count - count // 3
    share = factor.shape[0] // (count - late)

    def split_factor(n):
        rows = slice(n * share, (n + 1) * share)
        for k, part in enumerate(halves(factor[rows, :])):
            split[k, rows, :] = part
            store_factor(n, k).start()

    def store_factor(n, k):
        rows = slice(n * share, (n + 1) * share)
        first = k * factor.shape[0] + n * share
        return pltpu.make_async_copy(
            split.at[k, rows], factor_out.at[first : first + share], split_sems.at[n, k]
        )

    pattern_copy.wait()
    for r in range(rounds):
        for copy in loads(r):
            copy.wait()
        if r == 0:
            put(0, product(tall(dinv[0]), wide(rhs[:B, :])))
        low, high = max(bounds[r], 1), bounds[r + 1]
        prepare(low)
        for i in range(low, high):
            if i + 1 < high:
                prepare(i + 1)
            step(i)
            if i == late:
                factor_copy.wait()
            if i >= late:
                split_factor(i - late)
        store(r).start()
    upd_copy.wait()
    w[...] = -product(tall(upd[...]), solved[...])
    for r in range(rounds):
        store(r).wait()
    for n in range(count - late):
        for k in range(2):
            store_factor(n, k).wait()


def solve_subtree(rhs, dinv, off, pattern, upd, factor, rows):
    count = dinv.shape[0]
    bounds = [0, count // 6, count // 2, count]
    return pl.pallas_call(
        functools.partial(subtree_kernel, bounds),
        out_shape=(
            jax.ShapeDtypeStruct(rhs.shape, F32),
            jax.ShapeDtypeStruct((upd.shape[0], rhs.shape[1]), F32),
            pltpu.HBM((2 * rows, factor.shape[1]), BF16),
        ),
        in_specs=[HBM] * 6,
        out_specs=(HBM, VMEM, HBM),
        scratch_shapes=[
            pltpu.SMEM(pattern.shape, jnp.int32),
            pltpu.VMEM(rhs.shape, F32),
            pltpu.VMEM(dinv.shape, F32),
            pltpu.VMEM(off.shape, F32),
            pltpu.VMEM(upd.shape, F32),
            pltpu.VMEM(rhs.shape, F32),
            pltpu.VMEM((count, 2 * B, 2 * B), BF16),
            pltpu.VMEM((count, B, B), F32),
            pltpu.VMEM((count * B, 2 * B), BF16),
            pltpu.VMEM((rows, factor.shape[1]), F32),
            pltpu.VMEM((2, rows, factor.shape[1]), BF16),
            pltpu.SemaphoreType.DMA((len(bounds) - 1, 4)),
            pltpu.SemaphoreType.DMA((3,)),
            pltpu.SemaphoreType.DMA((count // 3, 2)),
        ],
        compiler_params=pltpu.CompilerParams(vmem_limit_bytes=40 * MIB),
        cost_estimate=pl.CostEstimate(flops=10**6, bytes_accessed=10**5, transcendentals=0),
        name="subtree",
    )(*[in_hbm(x) for x in (pattern, rhs, dinv, off, upd, factor)])


def exchange(x, mask):
    size = lax.axis_size("leaf") * lax.axis_size("front")
    return lax.ppermute(x, AXES, [(source, source ^ mask) for source in range(size)])


def spread(x, group, *throughs):
    masks = [0]
    apart = group // 2
    while apart >= 16:
        x = jnp.concatenate([x, exchange(x, apart)], 0)
        masks = masks + [mask ^ apart for mask in masks]
        apart //= 2
    low = 2 * apart
    arrays = [(mask, exchange(x, mask)) for mask in range(low - 2, 0, -2)]
    if low > 4:
        for n, through in enumerate(throughs):
            arrays[n] = (arrays[n][0], through(arrays[n][1]))
        arrays.append((0, x))
    else:
        arrays.append((0, throughs[0](x) if throughs else x))
    arrays += [(mask ^ 1, exchange(array, 1)) for mask, array in arrays]
    return [(array, [mask ^ high for high in masks]) for mask, array in arrays]


def factor_kernel(block, factor, own, out, own_out, held, sems):
    rows = held.shape[0]
    first, step = block[0] * block[1], held.shape[0] // sems.shape[0]
    loads = [
        pltpu.make_async_copy(
            factor.at[first + at : first + at + step], held.at[at : at + step], sems.at[at // step]
        )
        for at in range(0, rows, step)
    ]
    for load in loads:
        load.start()
    own_out[...] = own[...]
    for n, load in enumerate(loads):
        load.wait()
        high, low = halves(held[n * step : (n + 1) * step, :])
        out[n * step : (n + 1) * step, :] = high
        out[rows + n * step : rows + (n + 1) * step, :] = low


def prepare_factor(factor, block, own):
    rows, columns = block[1], factor.shape[1]
    return pl.pallas_call(
        functools.partial(factor_kernel, block),
        out_shape=(
            jax.ShapeDtypeStruct((2 * rows, columns), BF16),
            jax.ShapeDtypeStruct(own.shape, F32),
        ),
        in_specs=[HBM, VMEM],
        out_specs=(VMEM, VMEM),
        scratch_shapes=[
            pltpu.VMEM((rows, columns), F32),
            pltpu.SemaphoreType.DMA((max(1, min(4, rows // 16)),)),
        ],
        compiler_params=pltpu.CompilerParams(vmem_limit_bytes=16 * MIB),
        cost_estimate=pl.CostEstimate(
            flops=0, bytes_accessed=8 * rows * columns, transcendentals=0
        ),
        name="factor",
    )(in_hbm(factor), own)


def pivot_kernel(masks, shape, me, maps, *refs):
    count = len(masks)
    pieces, refs = refs[:count], refs[count:]
    own_h, refs = refs[: shape["h_count"]], refs[shape["h_count"] :]
    factor, refs = refs[0], refs[1:]
    earlier, refs = refs[: shape["earlier"]], refs[shape["earlier"] :]
    rides, rest = refs[: shape["rides"]], refs[shape["rides"] + shape["ahead"] :]
    front = shape["front"]
    p_size, child_rows, span = shape["p_size"], shape["child_rows"], shape["child_span"]
    upd_rows = shape["upd_rows"]
    device = me[0]
    frontal, right = rest[-2:]
    h_rows = p_size // shape["group"]
    for n, start, mask in shape["h_parts"]:
        rank = jnp.bitwise_and(jnp.bitwise_xor(device, mask), shape["group"] - 1)
        row = rank * h_rows
        part = own_h[n][start : start + h_rows, :]
        if h_rows >= B:
            frontal[pl.ds(row // B, h_rows // B)] = part.reshape(h_rows // B, B, -1)
        else:
            inner = pl.multiple_of(lax.rem(row, B), h_rows)
            frontal[row // B, pl.ds(inner, h_rows), :] = part
    if upd_rows:
        frontal[p_size // B :, :, :] = jnp.zeros_like(frontal[p_size // B :, :, :])
    if shape["earlier"]:
        done = 0
        for n, array in enumerate(earlier):
            rows = p_size // (front * 2**n)
            rest[0][done : done + rows, :] = array[:rows, :]
            done += rows
    step = min(child_rows, B)
    for piece, piece_masks in zip(pieces, masks, strict=True):
        for part, mask in enumerate(piece_masks):
            source = jnp.bitwise_xor(device, mask)
            if span:
                leaf = source // front
                row_of_map = shape["map_offset"] + leaf // span
                offset = (lax.rem(leaf, span) * front + lax.rem(source, front)) * child_rows
            else:
                row_of_map, offset = source, 0
            for at in range(0, child_rows, step):
                row = offset + at
                target = maps[row // B, row_of_map]
                inner = pl.multiple_of(lax.rem(row, B), step)
                here = part * child_rows + at
                if step == B:
                    frontal[target] += piece[here : here + step, :]
                else:
                    frontal[target, pl.ds(inner, step), :] += piece[here : here + step, :]
    right[...] = wide(frontal[: p_size // B].reshape(p_size, -1))
    z = product(factor[...], right[...])
    if shape["rides"]:
        rest[0][: z.shape[0], :] = z
        rest[0][z.shape[0] :, :] = rides[0][...]
    elif shape["earlier"]:
        rest[0][done : done + z.shape[0], :] = z
    else:
        rest[0][...] = z
    if upd_rows:
        rank = jnp.bitwise_and(device, shape["group"] - 1)
        row = rank * upd_rows
        if upd_rows >= B:
            side = frontal[pl.ds(p_size // B + row // B, upd_rows // B)]
            rest[1][...] = side.reshape(upd_rows, -1)
        else:
            inner = pl.multiple_of(lax.rem(row, B), upd_rows)
            rest[1][...] = frontal[p_size // B + row // B, pl.ds(inner, upd_rows), :]


def solve_pivots(me, maps, pieces, h, factor, earlier, rides, ahead, **shape):
    rows = factor.shape[0] // 2
    columns = pieces[0][0].shape[1]
    p_size = factor.shape[1]
    upd_rows = shape["upd_rows"]
    shape |= {
        "p_size": p_size,
        "earlier": len(earlier),
        "rides": len(rides),
        "ahead": len(ahead),
        "h_count": len(h[0]),
        "h_parts": h[1],
    }
    total = sum(p_size // (shape["front"] * 2**n) for n in range(len(earlier)))
    total += rows + sum(array.shape[0] for array in rides)
    outs = [jax.ShapeDtypeStruct((total, columns), F32)]
    if upd_rows:
        outs.append(jax.ShapeDtypeStruct((upd_rows, columns), F32))
    frontal_rows = p_size + upd_rows * shape["group"]
    operands = [array for array, _ in pieces] + h[0] + [factor, *earlier, *rides, *ahead]
    return pl.pallas_call(
        functools.partial(pivot_kernel, [masks for _, masks in pieces], shape),
        out_shape=tuple(outs),
        in_specs=[SMEM, SMEM] + [VMEM] * (len(operands) - len(ahead)) + [ANY] * len(ahead),
        out_specs=tuple(VMEM for _ in outs),
        scratch_shapes=[
            pltpu.VMEM((frontal_rows // B, B, columns), F32),
            pltpu.VMEM((p_size, 2 * columns), BF16),
        ],
        compiler_params=pltpu.CompilerParams(vmem_limit_bytes=24 * MIB),
        cost_estimate=pl.CostEstimate(
            flops=2 * rows * p_size * columns * 3, bytes_accessed=8 * 10**6, transcendentals=0
        ),
        name="pivots",
    )(me, maps, *operands)


def update_kernel(masks, group, me, *refs):
    count = len(masks)
    pieces = refs[:count]
    side, factor, w, right = refs[count:]
    rank = jnp.bitwise_and(me[0], group - 1)
    used = right.shape[0] // group
    for piece, piece_masks in zip(pieces, masks, strict=True):
        rows = piece.shape[0] // len(piece_masks)
        for part, mask in enumerate(piece_masks):
            source = jnp.bitwise_xor(rank, mask)
            where = pl.ds(pl.multiple_of(source * used, 16), used)
            right[where, :] = wide(piece[part * rows : part * rows + used, :])
    w[...] = side[...] - product(factor[...], right[...])


def solve_update(me, pieces, side, factor, group):
    rows, columns = side.shape
    p_size = factor.shape[1]
    return pl.pallas_call(
        functools.partial(update_kernel, [masks for _, masks in pieces], group),
        out_shape=jax.ShapeDtypeStruct((rows, columns), F32),
        in_specs=[SMEM] + [VMEM] * (len(pieces) + 2),
        out_specs=VMEM,
        scratch_shapes=[pltpu.VMEM((p_size, 2 * columns), BF16)],
        compiler_params=pltpu.CompilerParams(vmem_limit_bytes=24 * MIB),
        cost_estimate=pl.CostEstimate(
            flops=2 * rows * p_size * columns * 3, bytes_accessed=8 * 10**6, transcendentals=0
        ),
        name="update",
    )(me, *[array for array, _ in pieces], side, factor)


def join_kernel(plans, after, *refs):
    del after
    outs = refs[len(refs) - len(plans) :]
    for out, parts in zip(outs, plans, strict=True):
        at = 0
        for n, start, stop in parts:
            out[at : at + stop - start, :] = refs[n][start:stop, :]
            at += stop - start


def join_rows(after, arrays, plans):
    totals = [sum(stop - start for _, start, stop in parts) for parts in plans]
    return pl.pallas_call(
        functools.partial(join_kernel, plans),
        out_shape=tuple(
            jax.ShapeDtypeStruct((total, arrays[0].shape[1]), F32) for total in totals
        ),
        in_specs=[ANY] + [VMEM] * len(arrays),
        out_specs=tuple(VMEM for _ in totals),
        compiler_params=pltpu.CompilerParams(vmem_limit_bytes=8 * MIB),
        cost_estimate=pl.CostEstimate(flops=0, bytes_accessed=10**6, transcendentals=0),
        name="join",
    )(after, *arrays)


class Rhs:
    def __init__(self, front_rhs, p_size, groups):
        self.rows = [p_size // group for group in groups]
        self.masks = [0, 2]
        self.held = [front_rhs, exchange(front_rhs, 2)]
        self.spans = [front_rhs.shape[0]] * 2
        self.first = 0
        self.done = []
        root = front_rhs[front_rhs.shape[0] - self.rows[-1] :]
        self.root = [root, exchange(root, groups[-1] // 2)]

    def pair_root(self, after):
        plan = [(n, 0, self.rows[-1]) for n in range(2)]
        (self.root_pair,) = join_rows(after, self.root, [plan])

    def next_level(self, after):
        level = len(self.done)
        rows, group = self.rows[level], 2 * len(self.masks)
        rest = sum(self.rows[level + 1 : -1])
        parts = [
            (n, at + self.first)
            for n, (array, span) in enumerate(zip(self.held, self.spans, strict=True))
            for at in range(0, array.shape[0], span)
        ]
        plans = [[(n, at, at + rows) for n, at in parts]]
        if rest:
            plans.append([(n, at + rows, at + rows + rest) for n, at in parts])
        out = join_rows(after, self.held, plans)
        place = [(0, at * rows, mask) for at, mask in enumerate(self.masks)]
        place += [(1, at * rows, mask ^ 1) for at, mask in enumerate(self.masks)]
        self.done.append(([out[0], exchange(out[0], 1)], place))
        if rest:
            self.held = [out[1], exchange(out[1], group)]
            self.spans = [rest, rest]
            self.masks = self.masks + [mask ^ group for mask in self.masks]


def per_device(
    sub_rhs,
    sub_dinv,
    sub_off,
    sub_pattern,
    sub_update,
    sub_map,
    front_rhs,
    piv_inverse,
    upd_factor,
    front_map,
):
    front_size = lax.axis_size("front")
    leaf_size = lax.axis_size("leaf")
    level_count = leaf_size.bit_length()
    p_size = piv_inverse.shape[1]
    u_size = upd_factor.shape[0] * front_size * leaf_size // (2 * (leaf_size - 1))
    me = (lax.axis_index("leaf") * front_size + lax.axis_index("front")).reshape(1)

    size = front_size * leaf_size
    groups = [front_size * 2**level for level in range(level_count)]
    columns = sub_rhs.shape[1]
    sizes = [p_size // group for group in groups]
    rhs = Rhs(front_rhs, p_size, groups)

    kept = {}
    flat, update, kept["pivots"] = solve_subtree(
        sub_rhs, sub_dinv, sub_off, sub_pattern.T, sub_update, piv_inverse, sizes[0]
    )

    def keep(name, factor, block):
        def through(x):
            factor_rows, x = prepare_factor(factor, block, x)
            kept[name] = factor_rows
            return x

        return through

    pieces = spread(update, front_size)
    rhs.next_level(pieces[0][0])
    maps, map_offset, child_span = sub_map.T, 0, 0
    earlier = []
    for level in range(1, level_count + 1):
        group = groups[level - 1]
        last = level == level_count
        out = solve_pivots(
            me,
            maps,
            pieces,
            rhs.done[level - 1],
            kept["pivots"],
            earlier if last else [],
            [rhs.root_pair] if level == level_count - 1 else [],
            [rhs.root_pair] if level == 2 else [],
            front=front_size,
            child_rows=update.shape[0],
            child_span=child_span,
            map_offset=map_offset,
            upd_rows=0 if last else u_size // group,
            group=group,
        )
        if last:
            return flat, out[0]
        z, side = out
        earlier.append(z)
        if level > 1 and len(rhs.done) < level_count - 1:
            rhs.next_level(z)
        throughs = [keep("update", upd_factor, (2**level - 2, u_size // group))]
        following = [keep("pivots", piv_inverse, (2 ** (level + 1) - 2, sizes[level]))]
        if level == level_count - 1:
            throughs, following = throughs + following, []
        z_pieces = spread(z, group, *throughs)
        update = solve_update(me, z_pieces, side, kept["update"], group)
        pieces = spread(update, 2 * group, *following)
        if level == 1:
            rhs.pair_root(update)
        if level == 1:
            rhs.next_level(update)
        if level == level_count - 1:
            parts = []
            for n, (array, masks) in enumerate(z_pieces):
                rows = array.shape[0] // len(masks)
                for at, mask in enumerate(masks):
                    row = at * rows + sizes[level - 1]
                    parts.append((n, row, mask))
                    parts.append((n, row + sizes[level], mask ^ group))
            rhs.done.append(([array for array, _ in z_pieces], parts))
        map_offset = 0 if level == 1 else map_offset + leaf_size // child_span
        child_span = 2 ** (level - 1)
        maps = front_map.T


def solution(mesh):
    split = P(AXES)
    return jax.shard_map(
        per_device,
        mesh=mesh,
        in_specs=(split, split, split, split, split, P(), split, split, split, P()),
        out_specs=(split, split),
        check_vma=False,
    )
```

```python
import functools

import jax
import jax.numpy as jnp
from jax import lax
from jax.experimental import pallas as pl
from jax.experimental.pallas import tpu as pltpu
from jax.sharding import PartitionSpec as P

AXES = ("leaf", "front")
B = 128
BF16 = jnp.bfloat16
F32 = jnp.float32
ANY = pl.BlockSpec(memory_space=pl.ANY)
VMEM = pl.BlockSpec(memory_space=pltpu.VMEM)
HBM = pl.BlockSpec(memory_space=pltpu.HBM)
SMEM = pl.BlockSpec(memory_space=pltpu.SMEM)
MIB = 2**20


def in_hbm(x):
    return pltpu.with_memory_space_constraint(x, pltpu.HBM)


def in_vmem(x):
    return pltpu.with_memory_space_constraint(x, pltpu.VMEM)


def halves(x):
    high = x.astype(BF16)
    return high, (x - high.astype(F32)).astype(BF16)


def tall(x):
    return jnp.concatenate(halves(x), 0)


def wide(x):
    return jnp.concatenate(halves(x), 1)


def product(left, right):
    both = jnp.dot(left, right, preferred_element_type=F32)
    rows, cols = left.shape[0] // 2, right.shape[1] // 2
    return both[:rows, :cols] + both[:rows, cols:] + both[rows:, :cols]


def subtree_kernel(
    bounds, pattern_in, rhs_in, dinv_in, off_in, upd_in, factor_in, y_out, w, factor_out, *scratch
):
    pattern, rhs, dinv, off, upd, y, coef, lead, solved, factor, split, sems, end_sems, split_sems = scratch
    rounds = len(bounds) - 1

    def loads(r):
        low, high = bounds[r : r + 2]
        above = max(low - 1, 0)
        return [
            pltpu.make_async_copy(dinv_in.at[low:high], dinv.at[low:high], sems.at[r, 0]),
            pltpu.make_async_copy(
                rhs_in.at[low * B : high * B], rhs.at[low * B : high * B], sems.at[r, 1]
            ),
            pltpu.make_async_copy(
                off_in.at[above : high - 1], off.at[above : high - 1], sems.at[r, 2]
            ),
        ]

    def store(r):
        rows = slice(bounds[r] * B, bounds[r + 1] * B)
        return pltpu.make_async_copy(y.at[rows], y_out.at[rows], sems.at[r, 3])

    pattern_copy = pltpu.make_async_copy(pattern_in, pattern, end_sems.at[0])
    upd_copy = pltpu.make_async_copy(upd_in, upd, end_sems.at[1])
    factor_copy = pltpu.make_async_copy(
        factor_in.at[: factor.shape[0]], factor, end_sems.at[2]
    )
    pattern_copy.start()
    for r in range(rounds):
        for copy in loads(r):
            copy.start()
    upd_copy.start()
    factor_copy.start()

    def put(i, value):
        rows = slice(i * B, (i + 1) * B)
        y[rows, :] = value
        solved[rows, :] = wide(value)

    def prepare(i):
        right = jnp.concatenate([off[i - 1, 0], off[i - 1, 1], rhs[i * B : (i + 1) * B, :]], 1)
        out = product(tall(dinv[i]), wide(right))
        lead[i] = out[:, 2 * B :]
        coef[i] = tall(-out[:, : 2 * B])

    def step(i):
        first = pl.multiple_of(pattern[0, i - 1] * B, B)
        second = pl.multiple_of(pattern[1, i - 1] * B, B)
        known = jnp.concatenate([solved[pl.ds(first, B), :], solved[pl.ds(second, B), :]], 0)
        put(i, lead[i] + product(coef[i], known))

    count = dinv.shape[0]
    late = count - count // 3
    share = factor.shape[0] // (count - late)

    def split_factor(n):
        rows = slice(n * share, (n + 1) * share)
        for k, part in enumerate(halves(factor[rows, :])):
            split[k, rows, :] = part
            store_factor(n, k).start()

    def store_factor(n, k):
        rows = slice(n * share, (n + 1) * share)
        first = k * factor.shape[0] + n * share
        return pltpu.make_async_copy(
            split.at[k, rows], factor_out.at[first : first + share], split_sems.at[n, k]
        )

    pattern_copy.wait()
    for r in range(rounds):
        for copy in loads(r):
            copy.wait()
        if r == 0:
            put(0, product(tall(dinv[0]), wide(rhs[:B, :])))
        low, high = max(bounds[r], 1), bounds[r + 1]
        prepare(low)
        for i in range(low, high):
            if i + 1 < high:
                prepare(i + 1)
            step(i)
            if i == late:
                factor_copy.wait()
            if i >= late:
                split_factor(i - late)
        store(r).start()
    upd_copy.wait()
    w[...] = -product(tall(upd[...]), solved[...])
    for r in range(rounds):
        store(r).wait()
    for n in range(count - late):
        for k in range(2):
            store_factor(n, k).wait()


def solve_subtree(rhs, dinv, off, pattern, upd, factor, rows):
    count = dinv.shape[0]
    bounds = [0, count // 6, count // 2, count]
    return pl.pallas_call(
        functools.partial(subtree_kernel, bounds),
        out_shape=(
            jax.ShapeDtypeStruct(rhs.shape, F32),
            jax.ShapeDtypeStruct((upd.shape[0], rhs.shape[1]), F32),
            pltpu.HBM((2 * rows, factor.shape[1]), BF16),
        ),
        in_specs=[HBM] * 6,
        out_specs=(HBM, VMEM, HBM),
        scratch_shapes=[
            pltpu.SMEM(pattern.shape, jnp.int32),
            pltpu.VMEM(rhs.shape, F32),
            pltpu.VMEM(dinv.shape, F32),
            pltpu.VMEM(off.shape, F32),
            pltpu.VMEM(upd.shape, F32),
            pltpu.VMEM(rhs.shape, F32),
            pltpu.VMEM((count, 2 * B, 2 * B), BF16),
            pltpu.VMEM((count, B, B), F32),
            pltpu.VMEM((count * B, 2 * B), BF16),
            pltpu.VMEM((rows, factor.shape[1]), F32),
            pltpu.VMEM((2, rows, factor.shape[1]), BF16),
            pltpu.SemaphoreType.DMA((len(bounds) - 1, 4)),
            pltpu.SemaphoreType.DMA((3,)),
            pltpu.SemaphoreType.DMA((count // 3, 2)),
        ],
        compiler_params=pltpu.CompilerParams(vmem_limit_bytes=40 * MIB),
        cost_estimate=pl.CostEstimate(flops=10**6, bytes_accessed=10**5, transcendentals=0),
        name="subtree",
    )(*[in_hbm(x) for x in (pattern, rhs, dinv, off, upd, factor)])


def exchange(x, mask):
    size = lax.axis_size("leaf") * lax.axis_size("front")
    return lax.ppermute(x, AXES, [(source, source ^ mask) for source in range(size)])


def spread(x, group, *throughs):
    masks = [0]
    apart = group // 2
    while apart >= 16:
        x = jnp.concatenate([x, exchange(x, apart)], 0)
        masks = masks + [mask ^ apart for mask in masks]
        apart //= 2
    low = 2 * apart
    arrays = [(mask, exchange(x, mask)) for mask in range(low - 2, 0, -2)]
    if low > 4:
        for n, through in enumerate(throughs):
            arrays[n] = (arrays[n][0], through(arrays[n][1]))
        arrays.append((0, x))
    else:
        arrays.append((0, throughs[0](x) if throughs else x))
    arrays += [(mask ^ 1, exchange(array, 1)) for mask, array in arrays]
    return [(array, [mask ^ high for high in masks]) for mask, array in arrays]


def factor_kernel(block, factor, own, out, own_out, held, sems):
    rows = held.shape[0]
    first, step = block[0] * block[1], held.shape[0] // sems.shape[0]
    loads = [
        pltpu.make_async_copy(
            factor.at[first + at : first + at + step], held.at[at : at + step], sems.at[at // step]
        )
        for at in range(0, rows, step)
    ]
    for load in loads:
        load.start()
    own_out[...] = own[...]
    for n, load in enumerate(loads):
        load.wait()
        high, low = halves(held[n * step : (n + 1) * step, :])
        out[n * step : (n + 1) * step, :] = high
        out[rows + n * step : rows + (n + 1) * step, :] = low


def prepare_factor(factor, block, own):
    rows, columns = block[1], factor.shape[1]
    return pl.pallas_call(
        functools.partial(factor_kernel, block),
        out_shape=(
            jax.ShapeDtypeStruct((2 * rows, columns), BF16),
            jax.ShapeDtypeStruct(own.shape, F32),
        ),
        in_specs=[HBM, VMEM],
        out_specs=(VMEM, VMEM),
        scratch_shapes=[
            pltpu.VMEM((rows, columns), F32),
            pltpu.SemaphoreType.DMA((max(1, min(4, rows // 16)),)),
        ],
        compiler_params=pltpu.CompilerParams(vmem_limit_bytes=16 * MIB),
        cost_estimate=pl.CostEstimate(
            flops=0, bytes_accessed=8 * rows * columns, transcendentals=0
        ),
        name="factor",
    )(in_hbm(factor), own)


def pivot_kernel(masks, shape, me, maps, *refs):
    count = len(masks)
    pieces, refs = refs[:count], refs[count:]
    own_h, refs = refs[: shape["h_count"]], refs[shape["h_count"] :]
    factor, refs = refs[0], refs[1:]
    earlier, refs = refs[: shape["earlier"]], refs[shape["earlier"] :]
    rides, rest = refs[: shape["rides"]], refs[shape["rides"] + shape["ahead"] :]
    front = shape["front"]
    p_size, child_rows, span = shape["p_size"], shape["child_rows"], shape["child_span"]
    upd_rows = shape["upd_rows"]
    device = me[0]
    frontal, right = rest[-2:]
    h_rows = p_size // shape["group"]
    for n, start, mask in shape["h_parts"]:
        rank = jnp.bitwise_and(jnp.bitwise_xor(device, mask), shape["group"] - 1)
        row = rank * h_rows
        part = own_h[n][start : start + h_rows, :]
        if h_rows >= B:
            frontal[pl.ds(row // B, h_rows // B)] = part.reshape(h_rows // B, B, -1)
        else:
            inner = pl.multiple_of(lax.rem(row, B), h_rows)
            frontal[row // B, pl.ds(inner, h_rows), :] = part
    if upd_rows:
        frontal[p_size // B :, :, :] = jnp.zeros_like(frontal[p_size // B :, :, :])
    if shape["earlier"]:
        done = 0
        for n, array in enumerate(earlier):
            rows = p_size // (front * 2**n)
            rest[0][done : done + rows, :] = array[:rows, :]
            done += rows
    step = min(child_rows, B)
    for piece, piece_masks in zip(pieces, masks, strict=True):
        for part, mask in enumerate(piece_masks):
            source = jnp.bitwise_xor(device, mask)
            if span:
                leaf = source // front
                row_of_map = shape["map_offset"] + leaf // span
                offset = (lax.rem(leaf, span) * front + lax.rem(source, front)) * child_rows
            else:
                row_of_map, offset = source, 0
            for at in range(0, child_rows, step):
                row = offset + at
                target = maps[row // B, row_of_map]
                inner = pl.multiple_of(lax.rem(row, B), step)
                here = part * child_rows + at
                if step == B:
                    frontal[target] += piece[here : here + step, :]
                else:
                    frontal[target, pl.ds(inner, step), :] += piece[here : here + step, :]
    right[...] = wide(frontal[: p_size // B].reshape(p_size, -1))
    z = product(factor[...], right[...])
    if shape["rides"]:
        rest[0][: z.shape[0], :] = z
        rest[0][z.shape[0] :, :] = rides[0][...]
    elif shape["earlier"]:
        rest[0][done : done + z.shape[0], :] = z
    else:
        rest[0][...] = z
    if upd_rows:
        rank = jnp.bitwise_and(device, shape["group"] - 1)
        row = rank * upd_rows
        if upd_rows >= B:
            side = frontal[pl.ds(p_size // B + row // B, upd_rows // B)]
            rest[1][...] = side.reshape(upd_rows, -1)
        else:
            inner = pl.multiple_of(lax.rem(row, B), upd_rows)
            rest[1][...] = frontal[p_size // B + row // B, pl.ds(inner, upd_rows), :]


def solve_pivots(me, maps, pieces, h, factor, earlier, rides, ahead, **shape):
    rows = factor.shape[0] // 2
    columns = pieces[0][0].shape[1]
    p_size = factor.shape[1]
    upd_rows = shape["upd_rows"]
    shape |= {
        "p_size": p_size,
        "earlier": len(earlier),
        "rides": len(rides),
        "ahead": len(ahead),
        "h_count": len(h[0]),
        "h_parts": h[1],
    }
    total = sum(p_size // (shape["front"] * 2**n) for n in range(len(earlier)))
    total += rows + sum(array.shape[0] for array in rides)
    outs = [jax.ShapeDtypeStruct((total, columns), F32)]
    if upd_rows:
        outs.append(jax.ShapeDtypeStruct((upd_rows, columns), F32))
    frontal_rows = p_size + upd_rows * shape["group"]
    operands = [array for array, _ in pieces] + h[0] + [factor, *earlier, *rides, *ahead]
    return pl.pallas_call(
        functools.partial(pivot_kernel, [masks for _, masks in pieces], shape),
        out_shape=tuple(outs),
        in_specs=[SMEM, SMEM] + [VMEM] * (len(operands) - len(ahead)) + [ANY] * len(ahead),
        out_specs=tuple(VMEM for _ in outs),
        scratch_shapes=[
            pltpu.VMEM((frontal_rows // B, B, columns), F32),
            pltpu.VMEM((p_size, 2 * columns), BF16),
        ],
        compiler_params=pltpu.CompilerParams(vmem_limit_bytes=24 * MIB),
        cost_estimate=pl.CostEstimate(
            flops=2 * rows * p_size * columns * 3, bytes_accessed=8 * 10**6, transcendentals=0
        ),
        name="pivots",
    )(me, maps, *operands)


def update_kernel(masks, group, me, *refs):
    count = len(masks)
    pieces = refs[:count]
    side, factor, w, right = refs[count:]
    rank = jnp.bitwise_and(me[0], group - 1)
    used = right.shape[0] // group
    for piece, piece_masks in zip(pieces, masks, strict=True):
        rows = piece.shape[0] // len(piece_masks)
        for part, mask in enumerate(piece_masks):
            source = jnp.bitwise_xor(rank, mask)
            where = pl.ds(pl.multiple_of(source * used, 16), used)
            right[where, :] = wide(piece[part * rows : part * rows + used, :])
    w[...] = side[...] - product(factor[...], right[...])


def solve_update(me, pieces, side, factor, group):
    rows, columns = side.shape
    p_size = factor.shape[1]
    return pl.pallas_call(
        functools.partial(update_kernel, [masks for _, masks in pieces], group),
        out_shape=jax.ShapeDtypeStruct((rows, columns), F32),
        in_specs=[SMEM] + [VMEM] * (len(pieces) + 2),
        out_specs=VMEM,
        scratch_shapes=[pltpu.VMEM((p_size, 2 * columns), BF16)],
        compiler_params=pltpu.CompilerParams(vmem_limit_bytes=24 * MIB),
        cost_estimate=pl.CostEstimate(
            flops=2 * rows * p_size * columns * 3, bytes_accessed=8 * 10**6, transcendentals=0
        ),
        name="update",
    )(me, *[array for array, _ in pieces], side, factor)


def join_kernel(plans, after, *refs):
    del after
    outs = refs[len(refs) - len(plans) :]
    for out, parts in zip(outs, plans, strict=True):
        at = 0
        for n, start, stop in parts:
            out[at : at + stop - start, :] = refs[n][start:stop, :]
            at += stop - start


def join_rows(after, arrays, plans):
    totals = [sum(stop - start for _, start, stop in parts) for parts in plans]
    return pl.pallas_call(
        functools.partial(join_kernel, plans),
        out_shape=tuple(
            jax.ShapeDtypeStruct((total, arrays[0].shape[1]), F32) for total in totals
        ),
        in_specs=[ANY] + [VMEM] * len(arrays),
        out_specs=tuple(VMEM for _ in totals),
        compiler_params=pltpu.CompilerParams(vmem_limit_bytes=8 * MIB),
        cost_estimate=pl.CostEstimate(flops=0, bytes_accessed=10**6, transcendentals=0),
        name="join",
    )(after, *arrays)


class Rhs:
    def __init__(self, front_rhs, p_size, groups):
        self.rows = [p_size // group for group in groups]
        self.masks = [0, 2]
        self.held = [front_rhs, exchange(front_rhs, 2)]
        self.spans = [front_rhs.shape[0]] * 2
        self.first = 0
        self.done = []
        root = front_rhs[front_rhs.shape[0] - self.rows[-1] :]
        self.root = [root, exchange(root, groups[-1] // 2)]

    def pair_root(self, after):
        plan = [(n, 0, self.rows[-1]) for n in range(2)]
        (self.root_pair,) = join_rows(after, self.root, [plan])

    def next_level(self, after):
        level = len(self.done)
        rows, group = self.rows[level], 2 * len(self.masks)
        rest = sum(self.rows[level + 1 : -1])
        parts = [
            (n, at + self.first)
            for n, (array, span) in enumerate(zip(self.held, self.spans, strict=True))
            for at in range(0, array.shape[0], span)
        ]
        plans = [[(n, at, at + rows) for n, at in parts]]
        if rest:
            plans.append([(n, at + rows, at + rows + rest) for n, at in parts])
        out = join_rows(after, self.held, plans)
        place = [(0, at * rows, mask) for at, mask in enumerate(self.masks)]
        place += [(1, at * rows, mask ^ 1) for at, mask in enumerate(self.masks)]
        self.done.append(([out[0], exchange(out[0], 1)], place))
        if rest:
            self.held = [out[1], exchange(out[1], group)]
            self.spans = [rest, rest]
            self.masks = self.masks + [mask ^ group for mask in self.masks]


def per_device(
    sub_rhs,
    sub_dinv,
    sub_off,
    sub_pattern,
    sub_update,
    sub_map,
    front_rhs,
    piv_inverse,
    upd_factor,
    front_map,
):
    front_size = lax.axis_size("front")
    leaf_size = lax.axis_size("leaf")
    level_count = leaf_size.bit_length()
    p_size = piv_inverse.shape[1]
    u_size = upd_factor.shape[0] * front_size * leaf_size // (2 * (leaf_size - 1))
    me = (lax.axis_index("leaf") * front_size + lax.axis_index("front")).reshape(1)

    size = front_size * leaf_size
    groups = [front_size * 2**level for level in range(level_count)]
    columns = sub_rhs.shape[1]
    sizes = [p_size // group for group in groups]
    rhs = Rhs(front_rhs, p_size, groups)

    kept = {}
    flat, update, kept["pivots"] = solve_subtree(
        sub_rhs, sub_dinv, sub_off, sub_pattern.T, sub_update, piv_inverse, sizes[0]
    )

    def keep(name, factor, block):
        def through(x):
            factor_rows, x = prepare_factor(factor, block, x)
            kept[name] = factor_rows
            return x

        return through

    pieces = spread(update, front_size)
    rhs.next_level(pieces[0][0])
    maps, map_offset, child_span = sub_map.T, 0, 0
    earlier = []
    for level in range(1, level_count + 1):
        group = groups[level - 1]
        last = level == level_count
        out = solve_pivots(
            me,
            maps,
            pieces,
            rhs.done[level - 1],
            kept["pivots"],
            earlier if last else [],
            [rhs.root_pair] if level == level_count - 1 else [],
            [rhs.root_pair] if level == 2 else [],
            front=front_size,
            child_rows=update.shape[0],
            child_span=child_span,
            map_offset=map_offset,
            upd_rows=0 if last else u_size // group,
            group=group,
        )
        if last:
            return flat, out[0]
        z, side = out
        earlier.append(z)
        throughs = [keep("update", upd_factor, (2**level - 2, u_size // group))]
        following = [keep("pivots", piv_inverse, (2 ** (level + 1) - 2, sizes[level]))]
        if level == level_count - 1:
            throughs, following = throughs + following, []
        z_pieces = spread(z, group, *throughs)
        update = solve_update(me, z_pieces, side, kept["update"], group)
        pieces = spread(update, 2 * group, *following)
        if level == 1:
            rhs.pair_root(update)
        if level < level_count - 1:
            rhs.next_level(update)
        if level == level_count - 1:
            parts = []
            for n, (array, masks) in enumerate(z_pieces):
                rows = array.shape[0] // len(masks)
                for at, mask in enumerate(masks):
                    row = at * rows + sizes[level - 1]
                    parts.append((n, row, mask))
                    parts.append((n, row + sizes[level], mask ^ group))
            rhs.done.append(([array for array, _ in z_pieces], parts))
        map_offset = 0 if level == 1 else map_offset + leaf_size // child_span
        child_span = 2 ** (level - 1)
        maps = front_map.T


def solution(mesh):
    split = P(AXES)
    return jax.shard_map(
        per_device,
        mesh=mesh,
        in_specs=(split, split, split, split, split, P(), split, split, split, P()),
        out_specs=(split, split),
        check_vma=False,
    )
```
